128 devices in a mesh: dp: 16 (over y, z), tensor: 8 (over x, core).
Axes of the slice: x: 4, y: 4, z: 4, core: 2. Of those that a mesh axis runs over, the one named last changes fastest.
Arguments:
- queries: bfloat16 [3, 1536, 4096], P(None, 'dp', 'tensor'), may hold values from -88 to 88
- draft_keys: bfloat16 [3, 1536, 1024], P(None, 'dp', 'tensor'), may hold values from -5 to 5
- draft_values: bfloat16 [3, 1536, 1024], P(None, 'dp', 'tensor'), may hold values from -5 to 5
- key_cache: bfloat16 [1536, 256, 1024], P('dp', None, 'tensor'), may hold values from -4 to 4
- value_cache: bfloat16 [1536, 256, 1024], P('dp', None, 'tensor'), may hold values from -5 to 5
- lengths: int32 [1536], P('dp'), may hold values from 2 to 256, as said below
- request_adapter: int32 [1536], P('dp'), may hold values from 0 to 255, as said below
- adapter_page_table: int32 [256], replicated, may hold values from 0 to 255, as said below
- output_weight: bfloat16 [4096, 8192], P('tensor'), may hold values from -0.09375 to 0.09375
- adapter_down: bfloat16 [256, 32, 4096], P('dp', None, 'tensor'), may hold values from -0.09375 to 0.09375
- adapter_up: bfloat16 [256, 32, 8192], P('dp', None, 'tensor'), may hold values from -1 to 1
Outputs:
- layer_out: bfloat16 [3, 1536, 8192], P(None, 'dp', 'tensor')
The draws below stay inside these ranges and needn't reach their ends.
Inputs may be any that keep to these rules, and one draw needn't show every extreme that they name: A permutation: adapter a's factors are page adapter_page_table[a] of adapter_down and adapter_up, and page p lies with index p // 16 of dp. `request_adapter`: of the 96 requests of one index of dp, at most 12 use adapters whose pages one index of dp holds; one index of dp holds the pages of exactly 12 requests of every index of dp. `lengths`: some request has all 256 positions valid.
All inputs are finite; a program needn't handle non-finite values.
Results may differ from the reference program's by a relative error of at most 0.017.
Values may be sent and summed in bfloat16 or wider, within the bound.
No kernel may reach another device: no remote copies, remote signals or barrier semaphores. Data moves between devices by JAX's collectives and lax.ppermute only.
A program may use at most 192 MiB of HBM per device.

```python
import math
import jax
import jax.numpy as jnp
from jax import lax

MODEL_WIDTH = 8192
KVH = 8
HEAD_SIZE = 128
QUERY_HEADS = 32
ADAPTER_RANK = 32
DRAFT_STEPS = 3
ROW_DEV = 96
CACHE = 256
ADP_DEV = 16
ROWS = 1536
ADAPTER_PAGES = 256


def key_table(key):
    table_key = jax.random.fold_in(key, 11)
    return jax.random.truncated_normal(table_key, -4.0, 4.0, (ROWS, CACHE, KVH * HEAD_SIZE), jnp.float32)


def page_order(key):
    return jax.random.permutation(jax.random.fold_in(key, 17), ADAPTER_PAGES)


def draw_key_cache(key, part):
    key_values = key_table(key)
    return key_values.astype(jnp.bfloat16)


def draw_queries(key, part):
    key = jax.random.fold_in(key, 2)
    drawn = jax.random.truncated_normal(key, -4.0, 4.0, (DRAFT_STEPS, ROWS, QUERY_HEADS * HEAD_SIZE), jnp.float32)
    return drawn.astype(jnp.bfloat16)


def draw_lengths(key, part):
    key = jax.random.fold_in(key, 3)
    first_key, second_key = jax.random.split(key)
    drawn = jax.random.randint(first_key, (ROWS,), 2, CACHE + 1)
    chosen = jax.random.randint(second_key, (), 0, ROWS)
    return jnp.where(jnp.arange(ROWS) == chosen, CACHE, drawn).astype(jnp.int32)


def draw_adapter_page_table(key, part):
    ordering = page_order(key)
    return ordering.astype(jnp.int32)


def draw_request_adapter(key, part):
    ordering = page_order(key)
    key = jax.random.fold_in(key, 5)
    blocks = ROWS // ROW_DEV
    capacity = ROW_DEV // 8
    subkeys = jax.random.split(key, 4)
    busiest = jax.random.randint(subkeys[0], (), 0, blocks)
    offsets = jax.random.randint(subkeys[1], (blocks, 1), 0, blocks - 1)
    column = jnp.arange(ROW_DEV)[None, :]
    others = (busiest + 1 + (column - capacity + offsets) % (blocks - 1)) % blocks
    owner_of = jnp.where(column < capacity, busiest, others)
    shuffles = jax.vmap(lambda row_key: jax.random.permutation(row_key, ROW_DEV))(jax.random.split(subkeys[2], blocks))
    owner_of = jnp.take_along_axis(owner_of, shuffles, axis=1)
    slot_of = jax.random.randint(subkeys[3], (blocks, ROW_DEV), 0, ADP_DEV)
    page_of = (owner_of * ADP_DEV + slot_of).reshape(ROWS)
    inverse = jnp.argsort(ordering)
    return inverse[page_of].astype(jnp.int32)


def block_levels(own_key, extent, pieces, least, largest):
    factor_of = 1.0
    for axis_at, shards_of in pieces:
        heights = jax.random.uniform(jax.random.fold_in(jax.random.fold_in(own_key, 6), axis_at), (shards_of,), jnp.float32, least / len(pieces), largest / len(pieces))
        factor_of = factor_of * jnp.repeat(jnp.exp(heights), extent[axis_at] // shards_of).reshape((-1,) + (1,) * (len(extent) - 1 - axis_at))
    return factor_of


def bell_draw(rng, shape, deviation, most, cuts=(), kind=jnp.bfloat16):
    result = deviation * jax.random.normal(rng, shape, jnp.float32)
    if cuts:
        result = result * block_levels(rng, shape, cuts, -0.22, 0.18)
    return jnp.clip(result, -most, most).astype(kind)


def setup_inputs(seed: int = 0) -> dict:
    keys = jax.random.split(jax.random.key(seed), 12)
    return {
        "queries": draw_queries(jax.random.fold_in(keys[11], 71), 0),
        "draft_keys": bell_draw(keys[1], (DRAFT_STEPS, ROWS, KVH * HEAD_SIZE), 1.0, 5.0, ((1, 16), (2, 8))),
        "draft_values": bell_draw(keys[2], (DRAFT_STEPS, ROWS, KVH * HEAD_SIZE), 1.0, 5.0, ((1, 16), (2, 8))),
        "key_cache": draw_key_cache(jax.random.fold_in(keys[11], 71), 0),
        "value_cache": bell_draw(keys[4], (ROWS, CACHE, KVH * HEAD_SIZE), 1.0, 5.0, ((0, 16), (2, 8))),
        "lengths": draw_lengths(jax.random.fold_in(keys[11], 71), 0),
        "request_adapter": draw_request_adapter(jax.random.fold_in(keys[11], 71), 0),
        "adapter_page_table": draw_adapter_page_table(jax.random.fold_in(keys[11], 71), 0),
        "output_weight": bell_draw(keys[8], (QUERY_HEADS * HEAD_SIZE, MODEL_WIDTH), (QUERY_HEADS * HEAD_SIZE) ** -0.5, 0.09375, ((0, 8),)),
        "adapter_down": bell_draw(keys[9], (ADAPTER_PAGES, ADAPTER_RANK, QUERY_HEADS * HEAD_SIZE), (QUERY_HEADS * HEAD_SIZE) ** -0.5, 0.09375, ((0, 16), (2, 8))),
        "adapter_up": bell_draw(keys[10], (ADAPTER_PAGES, ADAPTER_RANK, MODEL_WIDTH), ADAPTER_RANK ** -0.5, 1.0, ((0, 16), (2, 8))),
    }


masked_score = -1e+30

def attend(queries, draft_keys, draft_values, key_cache, value_cache, lengths):
    draft_count, total_rows, q_width = queries.shape
    cache_len = key_cache.shape[1]
    kv_count = key_cache.shape[2] // HEAD_SIZE
    group_size = q_width // HEAD_SIZE // kv_count
    score_scale = 1.0 / math.sqrt(HEAD_SIZE)
    grouped = queries.astype(jnp.float32).reshape(draft_count, total_rows, kv_count, group_size, HEAD_SIZE)
    keys_cache = key_cache.astype(jnp.float32).reshape(total_rows, cache_len, kv_count, HEAD_SIZE)
    vals_cache = value_cache.astype(jnp.float32).reshape(total_rows, cache_len, kv_count, HEAD_SIZE)
    keys_new = draft_keys.astype(jnp.float32).reshape(draft_count, total_rows, kv_count, HEAD_SIZE)
    vals_new = draft_values.astype(jnp.float32).reshape(draft_count, total_rows, kv_count, HEAD_SIZE)
    cache_scores = jnp.einsum('sbkgd,blkd->sbkgl', grouped, keys_cache) * score_scale
    fresh_scores = jnp.einsum('sbkgd,tbkd->sbkgt', grouped, keys_new) * score_scale
    visible = jnp.arange(cache_len)[None, :] < lengths[:, None]
    cache_scores = jnp.where(visible[None, :, None, None, :], cache_scores, masked_score)
    causal = jnp.arange(draft_count)[:, None] >= jnp.arange(draft_count)[None, :]
    fresh_scores = jnp.where(causal[:, None, None, None, :], fresh_scores, masked_score)
    top_score = jnp.maximum(lax.optimization_barrier(jnp.max(cache_scores, axis=-1)), lax.optimization_barrier(jnp.max(fresh_scores, axis=-1)))[..., None]
    cache_exp = jnp.exp(cache_scores - top_score)
    fresh_exp = jnp.exp(fresh_scores - top_score)
    denom = lax.optimization_barrier(jnp.sum(cache_exp, axis=-1, keepdims=True)) + lax.optimization_barrier(jnp.sum(fresh_exp, axis=-1, keepdims=True))
    cache_weights = (cache_exp / denom).astype(jnp.bfloat16).astype(jnp.float32)
    fresh_weights = (fresh_exp / denom).astype(jnp.bfloat16).astype(jnp.float32)
    mixed = jnp.einsum('sbkgl,blkd->sbkgd', cache_weights, vals_cache)
    mixed = mixed + jnp.einsum('sbkgt,tbkd->sbkgd', fresh_weights, vals_new)
    return mixed.astype(jnp.bfloat16).reshape(draft_count, total_rows, q_width)

def reference(queries, draft_keys, draft_values, key_cache, value_cache, lengths, request_adapter, adapter_page_table, output_weight, adapter_down, adapter_up):
    page_index = adapter_page_table[request_adapter].astype(jnp.int32)
    block_row_span = ROW_DEV
    q_width = queries.shape[2]

    def take_rows(array, first_row, mesh_axis):
        return lax.dynamic_slice_in_dim(array, first_row, block_row_span, mesh_axis)

    def row_block(block_index):
        first_row = (block_index * block_row_span).astype(jnp.int32)
        attention_out = attend(take_rows(queries, first_row, 1), take_rows(draft_keys, first_row, 1), take_rows(draft_values, first_row, 1), take_rows(key_cache, first_row, 0), take_rows(value_cache, first_row, 0), take_rows(lengths, first_row, 0))
        base_projection = jnp.dot(attention_out.reshape(DRAFT_STEPS * block_row_span, q_width), output_weight, preferred_element_type=jnp.float32)
        block_adapter_pages = take_rows(page_index, first_row, 0)
        down_factor_rows = adapter_down[block_adapter_pages].astype(jnp.float32)
        rank_mixture = jnp.einsum('fzh,zgh->fzg', attention_out.astype(jnp.float32), down_factor_rows).astype(jnp.bfloat16)
        up_factor_rows = adapter_up[block_adapter_pages].astype(jnp.float32)
        adapter_term = jnp.einsum('tkv,kvq->tkq', rank_mixture.astype(jnp.float32), up_factor_rows).astype(jnp.bfloat16)
        final_output = base_projection.reshape(DRAFT_STEPS, block_row_span, MODEL_WIDTH) + adapter_term.astype(jnp.float32)
        return final_output.astype(jnp.bfloat16)
    blocks_out = lax.map(row_block, jnp.arange(ROWS // block_row_span, dtype=jnp.int32))
    return jnp.transpose(blocks_out, (1, 0, 2, 3)).reshape(DRAFT_STEPS, ROWS, MODEL_WIDTH)
```

```python
import functools, math
import jax, jax.numpy as jnp
from jax import lax
from jax.experimental import pallas as pl
from jax.experimental.pallas import tpu as pltpu
from jax.sharding import PartitionSpec as P

LANES = 128
STEP = 16
HALF = 8
VMEM = 63 * 1024 * 1024

def attend_kernel(slots, owner_rows, span, lengths, adapters, table, q, dk, dv, k, v, attn, payload, dest_out, kept):
    step = pl.program_id(0)
    drafts, _, width = q.shape
    cache = k.shape[1]
    heads = width // LANES
    rows = drafts * heads * HALF
    scale = math.log2(math.e) / math.sqrt(LANES)
    qf = q[...].astype(jnp.float32)
    dkf = dk[...].astype(jnp.float32)
    dvf = dv[...].astype(jnp.float32)
    sub = lax.broadcasted_iota(jnp.int32, (rows, cache), 0) % HALF
    lane8 = lax.broadcasted_iota(jnp.int32, (HALF, cache), 1)
    sub8 = lax.broadcasted_iota(jnp.int32, (HALF, cache), 0)
    drow = lax.broadcasted_iota(jnp.int32, (rows, drafts * HALF), 0)
    dlane = lax.broadcasted_iota(jnp.int32, (rows, drafts * HALF), 1)
    fresh_ok = (drow % HALF == dlane % HALF) & (dlane // HALF <= drow // (heads * HALF))
    outs = []
    for h in range(STEP // HALF):
        at = slice(h * HALF, (h + 1) * HALF)
        qb = jnp.concatenate([qf[s, at, g * LANES:(g + 1) * LANES] for s in range(drafts) for g in range(heads)], axis=0).astype(jnp.bfloat16)
        kb = jnp.concatenate([dkf[t, at] for t in range(drafts)], axis=0).astype(jnp.bfloat16)
        vb = jnp.concatenate([dvf[t, at] for t in range(drafts)], axis=0).astype(jnp.bfloat16)
        scores = None
        limit = jnp.zeros((HALF, cache), jnp.int32)
        for r in range(HALF):
            part = lax.dot_general(qb, k[h * HALF + r], (((1,), (1,)), ((), ())), preferred_element_type=jnp.float32)
            scores = part if r == 0 else jnp.where(sub == r, part, scores)
            limit = jnp.where(sub8 == r, lengths[step * STEP + h * HALF + r], limit)
        fresh = lax.dot_general(qb, kb, (((1,), (1,)), ((), ())), preferred_element_type=jnp.float32)
        seen = jnp.concatenate([(lane8 < limit).astype(jnp.int32)] * (drafts * heads), axis=0) > 0
        scores = jnp.where(seen, scores, -1e30)
        fresh = jnp.where(fresh_ok, fresh, -1e30)
        top = jnp.maximum(jnp.max(scores, axis=1, keepdims=True), jnp.max(fresh, axis=1, keepdims=True))
        e = jnp.exp2((scores - top) * scale)
        ef = jnp.exp2((fresh - top) * scale)
        total = jnp.sum(e, axis=1, keepdims=True) + jnp.sum(ef, axis=1, keepdims=True)
        inv = 1.0 / total
        w = e * inv
        wf = (ef * inv).astype(jnp.bfloat16)
        wide = jnp.concatenate([jnp.where(sub == r, w, 0.0).astype(jnp.bfloat16) for r in range(HALF)], axis=1)
        vals = v[h * HALF:(h + 1) * HALF].reshape(HALF * cache, LANES)
        mixed = jnp.dot(wide, vals, preferred_element_type=jnp.float32)
        mixed = mixed + jnp.dot(wf, vb, preferred_element_type=jnp.float32)
        outs.append(mixed)
    for s in range(drafts):
        for g in range(heads):
            at = (s * heads + g) * HALF
            piece = jnp.concatenate([o[at:at + HALF] for o in outs], axis=0).astype(jnp.bfloat16)
            attn[s, :, g * LANES:(g + 1) * LANES] = piece
            kept[s, pl.ds(pl.multiple_of(step * STEP, STEP), STEP), g * LANES:(g + 1) * LANES] = piece

    @pl.when(step == pl.num_programs(0) - 1)
    def _():
        count = adapters.shape[1]
        pages = table.shape[1]
        a = lax.broadcasted_iota(jnp.int32, (count, count), 0)
        b = lax.broadcasted_iota(jnp.int32, (count, count), 1)
        eye = a == b
        to_col = lambda row: jnp.sum(jnp.where(eye, jnp.broadcast_to(row, (count, count)), 0.0), axis=1, keepdims=True)
        to_row = lambda col: jnp.sum(jnp.where(eye, jnp.broadcast_to(col, (count, count)), 0.0), axis=0, keepdims=True)
        acol = to_col(adapters[...].astype(jnp.float32)).astype(jnp.int32)
        hit = acol == lax.broadcasted_iota(jnp.int32, (count, pages), 1)
        page = jnp.sum(jnp.where(hit, jnp.broadcast_to(table[...].astype(jnp.float32), (count, pages)), 0.0), axis=1, keepdims=True)
        prow = to_row(page).astype(jnp.int32)
        pcol = page.astype(jnp.int32)
        orow, ocol = prow // span, pcol // span
        rank = jnp.sum(jnp.where((ocol == orow) & (a < b), 1.0, 0.0), axis=0, keepdims=True).astype(jnp.int32)
        dest = orow * owner_rows + rank
        dest_col = jnp.sum(jnp.where((ocol == orow) & (b < a), 1.0, 0.0), axis=1, keepdims=True).astype(jnp.int32)
        dest_out[...] = jnp.broadcast_to(ocol * owner_rows + dest_col, dest_out.shape)
        place = lax.broadcasted_iota(jnp.int32, (payload.shape[0], count), 0)
        local = jnp.broadcast_to((pcol - ocol * span).astype(jnp.float32), (count, LANES)).astype(jnp.bfloat16)
        acc = None
        for s in range(drafts):
            pick = jnp.where(place == dest + s * slots, 1.0, 0.0).astype(jnp.bfloat16)
            rowsv = jnp.concatenate([kept[s], local], axis=1)
            part = jnp.dot(pick, rowsv, preferred_element_type=jnp.float32)
            acc = part if acc is None else acc + part
        payload[...] = acc.astype(jnp.bfloat16)

def attend(queries, draft_keys, draft_values, key_cache, value_cache, lengths, request_adapter, table, slots, owner_rows, owners, span):
    drafts, rows, width = queries.shape
    cache = key_cache.shape[1]
    return pl.pallas_call(
        functools.partial(attend_kernel, slots, owner_rows, span),
        grid=(rows // STEP,),
        in_specs=[
            pl.BlockSpec(memory_space=pltpu.SMEM),
            pl.BlockSpec((1, rows), lambda i: (0, 0)),
            pl.BlockSpec((1, table.shape[0]), lambda i: (0, 0)),
            pl.BlockSpec((drafts, STEP, width), lambda i: (0, i, 0)),
            pl.BlockSpec((drafts, STEP, LANES), lambda i: (0, i, 0)),
            pl.BlockSpec((drafts, STEP, LANES), lambda i: (0, i, 0)),
            pl.BlockSpec((STEP, cache, LANES), lambda i: (i, 0, 0)),
            pl.BlockSpec((STEP, cache, LANES), lambda i: (i, 0, 0)),
        ],
        out_specs=[
            pl.BlockSpec((drafts, STEP, width), lambda i: (0, i, 0)),
            pl.BlockSpec((owners * owner_rows, width + LANES), lambda i: (0, 0)),
            pl.BlockSpec((rows, LANES), lambda i: (0, 0)),
        ],
        out_shape=[
            jax.ShapeDtypeStruct((drafts, rows, width), jnp.bfloat16),
            jax.ShapeDtypeStruct((owners * owner_rows, width + LANES), jnp.bfloat16),
            jax.ShapeDtypeStruct((rows, LANES), jnp.int32),
        ],
        scratch_shapes=[pltpu.VMEM((drafts, rows, width), jnp.bfloat16)],
        compiler_params=pltpu.CompilerParams(vmem_limit_bytes=VMEM),
        name="attend",
    )(lengths, request_adapter.reshape(1, rows), table.reshape(1, -1), queries, draft_keys, draft_values, key_cache, value_cache)


def base_kernel(attn, weight, out):
    drafts, rows, width = attn.shape
    out[0] = jnp.dot(
        attn[...].reshape(drafts * rows, width), weight[...], preferred_element_type=jnp.float32
    ).astype(jnp.bfloat16)


def project(attn, weight, parts):
    drafts, rows, width = attn.shape
    part = weight.shape[1] // parts
    return pl.pallas_call(
        base_kernel,
        grid=(parts,),
        in_specs=[
            pl.BlockSpec((drafts, rows, width), lambda j: (0, 0, 0)),
            pl.BlockSpec((width, part), lambda j: (0, j)),
        ],
        out_specs=pl.BlockSpec((1, drafts * rows, part), lambda j: (j, 0, 0)),
        out_shape=jax.ShapeDtypeStruct((parts, drafts * rows, part), jnp.bfloat16),
        compiler_params=pltpu.CompilerParams(vmem_limit_bytes=VMEM),
        name="project",
    )(attn, weight)


def down_kernel(arrived, down, mix):
    width = down.shape[1]
    span = down.shape[0] // mix.shape[0]
    product = lax.dot_general(
        down[...], arrived[:, :width], (((1,), (1,)), ((), ())), preferred_element_type=jnp.float32
    )
    ones = jnp.ones((8, LANES), jnp.bfloat16)
    page = lax.dot_general(
        ones, arrived[:, width:], (((1,), (1,)), ((), ())), preferred_element_type=jnp.float32
    )[:1] * (1.0 / LANES)
    rank = mix.shape[0]
    total = jnp.zeros(mix.shape, jnp.float32)
    for p in range(span):
        total = total + jnp.where(page == float(p), product[p * rank:(p + 1) * rank], 0.0)
    mix[...] = total


def down_mix(arrived, down):
    rows = arrived.shape[0]
    span, rank, width = down.shape
    return pl.pallas_call(
        down_kernel,
        out_shape=jax.ShapeDtypeStruct((rank, rows), jnp.float32),
        compiler_params=pltpu.CompilerParams(vmem_limit_bytes=VMEM),
        name="down_mix",
    )(arrived, down.reshape(span * rank, width))


def up_kernel(mine, one, two, three, arrived, up, out):
    rank = mine.shape[0]
    spread_width = up.shape[0]
    mix = (
        mine[...].astype(jnp.float32)
        + one[...].astype(jnp.float32)
        + two[...].astype(jnp.float32)
        + three[...].astype(jnp.float32)
    ).astype(jnp.bfloat16)
    a = lax.broadcasted_iota(jnp.int32, (rank, spread_width), 0)
    b = lax.broadcasted_iota(jnp.int32, (rank, spread_width), 1)
    repeat = jnp.where(b % rank == a, 1.0, 0.0).astype(jnp.bfloat16)
    spread = lax.dot_general(
        mix, repeat, (((0,), (0,)), ((), ())), preferred_element_type=jnp.float32
    )
    meta = arrived[...].astype(jnp.float32)
    pieces = []
    for j in range(spread_width // LANES):
        lane = lax.broadcasted_iota(jnp.int32, meta.shape, 1) + j * LANES
        same = meta == (lane // rank).astype(jnp.float32)
        pieces.append(jnp.where(same, spread[:, j * LANES:(j + 1) * LANES], 0.0).astype(jnp.bfloat16))
    out[...] = jnp.dot(
        jnp.concatenate(pieces, axis=1), up[...], preferred_element_type=jnp.float32
    ).astype(jnp.bfloat16)


def up_terms(mixes, arrived, up):
    rows, full = arrived.shape
    span, rank, width = up.shape
    mix_spec = pl.BlockSpec((rank, rows), lambda i: (0, 0))
    return pl.pallas_call(
        up_kernel,
        grid=(1,),
        in_specs=[mix_spec] * 4
        + [
            pl.BlockSpec((rows, LANES), lambda i: (0, full // LANES - 1)),
            pl.BlockSpec((span * rank, width), lambda i: (0, 0)),
        ],
        out_specs=pl.BlockSpec((rows, width), lambda i: (0, 0)),
        out_shape=jax.ShapeDtypeStruct((rows, width), jnp.bfloat16),
        compiler_params=pltpu.CompilerParams(vmem_limit_bytes=VMEM),
        name="up_terms",
    )(*mixes, arrived, up.reshape(span * rank, width))


def finish_kernel(slots, base, terms, dest, out):
    drafts, rows, width = out.shape
    places = terms.shape[0]
    lane = lax.broadcasted_iota(jnp.int32, (rows, places), 1)
    where_to = dest[:, :1]
    for s in range(drafts):
        pick = jnp.where(lane == where_to + s * slots, 1.0, 0.0).astype(jnp.bfloat16)
        term = jnp.dot(pick, terms[...], preferred_element_type=jnp.float32)
        out[s] = (base[s * rows:(s + 1) * rows].astype(jnp.float32) + term).astype(jnp.bfloat16)


def finish(base, terms, dest, drafts, slots):
    rows = dest.shape[0]
    width = base.shape[1]
    return pl.pallas_call(
        functools.partial(finish_kernel, slots),
        out_shape=jax.ShapeDtypeStruct((drafts, rows, width), jnp.bfloat16),
        compiler_params=pltpu.CompilerParams(vmem_limit_bytes=VMEM),
        name="finish",
    )(base, terms, dest)


def body(
    queries,
    draft_keys,
    draft_values,
    key_cache,
    value_cache,
    lengths,
    request_adapter,
    adapter_page_table,
    output_weight,
    adapter_down,
    adapter_up,
):
    drafts, rows, width = queries.shape
    owners = lax.axis_size("dp")
    parts = lax.axis_size("tensor")
    span, rank, _ = adapter_down.shape
    slots = rows // 8
    owner_rows = -(-drafts * slots // 8) * 8
    attn, payload, dest = attend(
        queries, draft_keys, draft_values, key_cache, value_cache, lengths, request_adapter,
        adapter_page_table, slots, owner_rows, owners, span,
    )
    partial_base = project(attn, output_weight, parts)
    base = lax.psum_scatter(partial_base, "tensor", scatter_dimension=0, tiled=False)
    arrived = lax.all_to_all(
        payload.reshape(owners, owner_rows, -1), "dp", 0, 0, tiled=True
    ).reshape(owners * owner_rows, -1)
    mine = down_mix(arrived, adapter_down)
    chips = parts // 2
    other = lax.ppermute(mine, "tensor", [(i, i ^ 1) for i in range(parts)])
    pair = (mine + other).astype(jnp.bfloat16)
    mixes = [pair] + [
        lax.ppermute(pair, "tensor", [(2 * x + c, 2 * ((x + k) % chips) + c) for x in range(chips) for c in range(2)])
        for k in range(1, chips)
    ]
    terms = up_terms(mixes, arrived, adapter_up)
    terms = lax.all_to_all(
        terms.reshape(owners, owner_rows, -1), "dp", 0, 0, tiled=True
    ).reshape(owners * owner_rows, -1)
    return finish(base, terms, dest, drafts, slots)


def solution(mesh):
    placed = (
        P(None, "dp", "tensor"),
        P(None, "dp", "tensor"),
        P(None, "dp", "tensor"),
        P("dp", None, "tensor"),
        P("dp", None, "tensor"),
        P("dp"),
        P("dp"),
        P(),
        P("tensor", None),
        P("dp", None, "tensor"),
        P("dp", None, "tensor"),
    )
    return jax.shard_map(
        body, mesh=mesh, in_specs=placed, out_specs=P(None, "dp", "tensor"), check_vma=False
    )
```

```python
import functools, math
import jax, jax.numpy as jnp
from jax import lax
from jax.experimental import pallas as pl
from jax.experimental.pallas import tpu as pltpu
from jax.sharding import PartitionSpec as P

LANES = 128
STEP = 16
HALF = 8
AHEAD = (2, 1, 3, 0)
VMEM = 63 * 1024 * 1024

def attend_kernel(slots, owner_rows, span, lengths, adapters, table, q, dk, dv, k, v, attn, payload, dest_out, kept):
    step = pl.program_id(0)
    drafts, _, width = q.shape
    cache = k.shape[1]
    heads = width // LANES
    rows = drafts * heads * HALF
    scale = math.log2(math.e) / math.sqrt(LANES)
    qf = q[...].astype(jnp.float32)
    dkf = dk[...].astype(jnp.float32)
    dvf = dv[...].astype(jnp.float32)
    sub = lax.broadcasted_iota(jnp.int32, (rows, cache), 0) % HALF
    lane8 = lax.broadcasted_iota(jnp.int32, (HALF, cache), 1)
    sub8 = lax.broadcasted_iota(jnp.int32, (HALF, cache), 0)
    drow = lax.broadcasted_iota(jnp.int32, (rows, drafts * HALF), 0)
    dlane = lax.broadcasted_iota(jnp.int32, (rows, drafts * HALF), 1)
    fresh_ok = (drow % HALF == dlane % HALF) & (dlane // HALF <= drow // (heads * HALF))
    outs = []
    for h in range(STEP // HALF):
        at = slice(h * HALF, (h + 1) * HALF)
        qb = jnp.concatenate([qf[s, at, g * LANES:(g + 1) * LANES] for s in range(drafts) for g in range(heads)], axis=0).astype(jnp.bfloat16)
        kb = jnp.concatenate([dkf[t, at] for t in range(drafts)], axis=0).astype(jnp.bfloat16)
        vb = jnp.concatenate([dvf[t, at] for t in range(drafts)], axis=0).astype(jnp.bfloat16)
        scores = None
        limit = jnp.zeros((HALF, cache), jnp.int32)
        for r in range(HALF):
            part = lax.dot_general(qb, k[h * HALF + r], (((1,), (1,)), ((), ())), preferred_element_type=jnp.float32)
            scores = part if r == 0 else jnp.where(sub == r, part, scores)
            limit = jnp.where(sub8 == r, lengths[step * STEP + h * HALF + r], limit)
        fresh = lax.dot_general(qb, kb, (((1,), (1,)), ((), ())), preferred_element_type=jnp.float32)
        seen = jnp.concatenate([(lane8 < limit).astype(jnp.int32)] * (drafts * heads), axis=0) > 0
        scores = jnp.where(seen, scores, -1e30)
        fresh = jnp.where(fresh_ok, fresh, -1e30)
        top = jnp.maximum(jnp.max(scores, axis=1, keepdims=True), jnp.max(fresh, axis=1, keepdims=True))
        e = jnp.exp2((scores - top) * scale)
        ef = jnp.exp2((fresh - top) * scale)
        total = jnp.sum(e, axis=1, keepdims=True) + jnp.sum(ef, axis=1, keepdims=True)
        inv = 1.0 / total
        w = e * inv
        wf = (ef * inv).astype(jnp.bfloat16)
        wide = jnp.concatenate([jnp.where(sub == r, w, 0.0).astype(jnp.bfloat16) for r in range(HALF)], axis=1)
        vals = v[h * HALF:(h + 1) * HALF].reshape(HALF * cache, LANES)
        mixed = jnp.dot(wide, vals, preferred_element_type=jnp.float32)
        mixed = mixed + jnp.dot(wf, vb, preferred_element_type=jnp.float32)
        outs.append(mixed)
    for s in range(drafts):
        for g in range(heads):
            at = (s * heads + g) * HALF
            piece = jnp.concatenate([o[at:at + HALF] for o in outs], axis=0).astype(jnp.bfloat16)
            attn[s, :, g * LANES:(g + 1) * LANES] = piece
            kept[s, pl.ds(pl.multiple_of(step * STEP, STEP), STEP), g * LANES:(g + 1) * LANES] = piece

    @pl.when(step == pl.num_programs(0) - 1)
    def _():
        count = adapters.shape[1]
        pages = table.shape[1]
        a = lax.broadcasted_iota(jnp.int32, (count, count), 0)
        b = lax.broadcasted_iota(jnp.int32, (count, count), 1)
        eye = a == b
        to_col = lambda row: jnp.sum(jnp.where(eye, jnp.broadcast_to(row, (count, count)), 0.0), axis=1, keepdims=True)
        to_row = lambda col: jnp.sum(jnp.where(eye, jnp.broadcast_to(col, (count, count)), 0.0), axis=0, keepdims=True)
        acol = to_col(adapters[...].astype(jnp.float32)).astype(jnp.int32)
        hit = acol == lax.broadcasted_iota(jnp.int32, (count, pages), 1)
        page = jnp.sum(jnp.where(hit, jnp.broadcast_to(table[...].astype(jnp.float32), (count, pages)), 0.0), axis=1, keepdims=True)
        prow = to_row(page).astype(jnp.int32)
        pcol = page.astype(jnp.int32)
        orow, ocol = prow // span, pcol // span
        rank = jnp.sum(jnp.where((ocol == orow) & (a < b), 1.0, 0.0), axis=0, keepdims=True).astype(jnp.int32)
        dest = orow * owner_rows + rank
        dest_col = jnp.sum(jnp.where((ocol == orow) & (b < a), 1.0, 0.0), axis=1, keepdims=True).astype(jnp.int32)
        dest_out[...] = jnp.broadcast_to(ocol * owner_rows + dest_col, dest_out.shape)
        place = lax.broadcasted_iota(jnp.int32, (payload.shape[0], count), 0)
        local = jnp.broadcast_to((pcol - ocol * span).astype(jnp.float32), (count, LANES)).astype(jnp.bfloat16)
        acc = None
        for s in range(drafts):
            pick = jnp.where(place == dest + s * slots, 1.0, 0.0).astype(jnp.bfloat16)
            rowsv = jnp.concatenate([kept[s], local], axis=1)
            part = jnp.dot(pick, rowsv, preferred_element_type=jnp.float32)
            acc = part if acc is None else acc + part
        payload[...] = acc.astype(jnp.bfloat16)

def attend(queries, draft_keys, draft_values, key_cache, value_cache, lengths, request_adapter, table, slots, owner_rows, owners, span):
    drafts, rows, width = queries.shape
    cache = key_cache.shape[1]
    return pl.pallas_call(
        functools.partial(attend_kernel, slots, owner_rows, span),
        grid=(rows // STEP,),
        in_specs=[
            pl.BlockSpec(memory_space=pltpu.SMEM),
            pl.BlockSpec((1, rows), lambda i: (0, 0)),
            pl.BlockSpec((1, table.shape[0]), lambda i: (0, 0)),
            pl.BlockSpec((drafts, STEP, width), lambda i: (0, i, 0)),
            pl.BlockSpec((drafts, STEP, LANES), lambda i: (0, i, 0)),
            pl.BlockSpec((drafts, STEP, LANES), lambda i: (0, i, 0)),
            pl.BlockSpec((STEP, cache, LANES), lambda i: (i, 0, 0)),
            pl.BlockSpec((STEP, cache, LANES), lambda i: (i, 0, 0)),
        ],
        out_specs=[
            pl.BlockSpec((drafts, STEP, width), lambda i: (0, i, 0)),
            pl.BlockSpec((owners * owner_rows, width + LANES), lambda i: (0, 0)),
            pl.BlockSpec((rows, LANES), lambda i: (0, 0)),
        ],
        out_shape=[
            jax.ShapeDtypeStruct((drafts, rows, width), jnp.bfloat16),
            jax.ShapeDtypeStruct((owners * owner_rows, width + LANES), jnp.bfloat16),
            jax.ShapeDtypeStruct((rows, LANES), jnp.int32),
        ],
        scratch_shapes=[pltpu.VMEM((drafts, rows, width), jnp.bfloat16)],
        compiler_params=pltpu.CompilerParams(vmem_limit_bytes=VMEM),
        cost_estimate=pl.CostEstimate(
            flops=8 * queries.size * cache, bytes_accessed=4 * key_cache.size, transcendentals=0
        ),
        name="attend",
    )(lengths, request_adapter.reshape(1, rows), table.reshape(1, -1), queries, draft_keys, draft_values, key_cache, value_cache)


def fetch_blocks(weight, held, sems, other_core):
    place = lax.axis_index("tensor")
    chips, _, part = held.shape
    core = place % 2
    core = 1 - core if other_core else core
    fetches = []
    for j, ahead in enumerate(AHEAD):
        block = (place // 2 + ahead) % chips * 2 + core
        fetches.append(
            pltpu.make_async_copy(
                weight.at[:, pl.ds(pl.multiple_of(block * part, part), part)], held.at[j], sems.at[j]
            )
        )
        fetches[-1].start()
    return fetches


def sent_kernel(attn, weight, out, held, sems):
    drafts, rows, width = attn.shape
    fetches = fetch_blocks(weight, held, sems, True)
    flat = attn[...].reshape(drafts * rows, width)
    for j, fetch in enumerate(fetches):
        fetch.wait()
        out[j] = jnp.dot(flat, held[j], preferred_element_type=jnp.float32).astype(jnp.bfloat16)


def kept_kernel(attn, weight, other, far_up, far_down, up, down, own, held, sems):
    drafts, rows, width = attn.shape
    half = drafts * rows // 2
    fetches = fetch_blocks(weight, held, sems, False)
    flat = attn[...].reshape(drafts * rows, width)
    for j, fetch in enumerate(fetches):
        fetch.wait()
        total = jnp.dot(flat, held[j], preferred_element_type=jnp.float32)
        total = (total + other[j].astype(jnp.float32)).astype(jnp.bfloat16)
        if j == 0:
            far_up[...] = total[:half]
            far_down[...] = total[half:]
        else:
            (up, down, own)[j - 1][...] = total


def project(attn, weight, other, parts):
    drafts, rows, width = attn.shape
    part = weight.shape[1] // parts
    chips = parts // 2
    full = (drafts * rows, part)
    half = (drafts * rows // 2, part)
    shapes = [(chips,) + full] if other is None else [half, half, full, full, full]
    ins = [attn, weight] + ([] if other is None else [other])
    vmem = pl.BlockSpec(memory_space=pltpu.VMEM)
    return pl.pallas_call(
        sent_kernel if other is None else kept_kernel,
        in_specs=[vmem, pl.BlockSpec(memory_space=pltpu.HBM)] + [vmem] * (len(ins) - 2),
        out_specs=[vmem] * len(shapes),
        out_shape=[jax.ShapeDtypeStruct(s, jnp.bfloat16) for s in shapes],
        scratch_shapes=[
            pltpu.VMEM((chips, width, part), jnp.bfloat16),
            pltpu.SemaphoreType.DMA((chips,)),
        ],
        compiler_params=pltpu.CompilerParams(vmem_limit_bytes=VMEM * 8 // 9),
        cost_estimate=pl.CostEstimate(flops=1, bytes_accessed=1, transcendentals=0),
        name="project_sent" if other is None else "project_kept",
    )(*ins)


def merge_kernel(up, down, far_up, far_down, up_out, down_out):
    half = far_up.shape[0]
    add = lambda a, b: (a.astype(jnp.float32) + b.astype(jnp.float32)).astype(jnp.bfloat16)
    up_out[:half] = add(up[:half], far_up[...])
    up_out[half:] = up[half:]
    down_out[:half] = down[:half]
    down_out[half:] = add(down[half:], far_down[...])


def merge(up, down, far_up, far_down):
    shape = jax.ShapeDtypeStruct(up.shape, up.dtype)
    return pl.pallas_call(
        merge_kernel,
        out_shape=[shape, shape],
        compiler_params=pltpu.CompilerParams(vmem_limit_bytes=VMEM // 4),
        cost_estimate=pl.CostEstimate(flops=0, bytes_accessed=10 * up.size, transcendentals=0),
        name="merge",
    )(up, down, far_up, far_down)


def down_kernel(arrived, down, mix):
    width = down.shape[1]
    span = down.shape[0] // mix.shape[0]
    product = lax.dot_general(
        down[...], arrived[:, :width], (((1,), (1,)), ((), ())), preferred_element_type=jnp.float32
    )
    ones = jnp.ones((8, LANES), jnp.bfloat16)
    page = lax.dot_general(
        ones, arrived[:, width:], (((1,), (1,)), ((), ())), preferred_element_type=jnp.float32
    )[:1] * (1.0 / LANES)
    rank = mix.shape[0]
    total = jnp.zeros(mix.shape, jnp.float32)
    for p in range(span):
        total = total + jnp.where(page == float(p), product[p * rank:(p + 1) * rank], 0.0)
    mix[...] = total


def down_mix(arrived, down):
    rows = arrived.shape[0]
    span, rank, width = down.shape
    return pl.pallas_call(
        down_kernel,
        out_shape=jax.ShapeDtypeStruct((rank, rows), jnp.float32),
        compiler_params=pltpu.CompilerParams(vmem_limit_bytes=VMEM // 4),
        cost_estimate=pl.CostEstimate(flops=2 * rows * down.size, bytes_accessed=2 * (arrived.size + down.size), transcendentals=0),
        name="down_mix",
    )(arrived, down.reshape(span * rank, width))


def up_kernel(mine, one, two, three, arrived, up, out):
    rank = mine.shape[0]
    spread_width = up.shape[0]
    mix = (
        mine[...].astype(jnp.float32)
        + one[...].astype(jnp.float32)
        + two[...].astype(jnp.float32)
        + three[...].astype(jnp.float32)
    ).astype(jnp.bfloat16)
    a = lax.broadcasted_iota(jnp.int32, (rank, spread_width), 0)
    b = lax.broadcasted_iota(jnp.int32, (rank, spread_width), 1)
    repeat = jnp.where(b % rank == a, 1.0, 0.0).astype(jnp.bfloat16)
    spread = lax.dot_general(
        mix, repeat, (((0,), (0,)), ((), ())), preferred_element_type=jnp.float32
    )
    meta = arrived[...].astype(jnp.float32)
    pieces = []
    for j in range(spread_width // LANES):
        lane = lax.broadcasted_iota(jnp.int32, meta.shape, 1) + j * LANES
        same = meta == (lane // rank).astype(jnp.float32)
        pieces.append(jnp.where(same, spread[:, j * LANES:(j + 1) * LANES], 0.0).astype(jnp.bfloat16))
    out[...] = jnp.dot(
        jnp.concatenate(pieces, axis=1), up[...], preferred_element_type=jnp.float32
    ).astype(jnp.bfloat16)


def up_terms(mixes, arrived, up):
    rows, full = arrived.shape
    span, rank, width = up.shape
    mix_spec = pl.BlockSpec((rank, rows), lambda i: (0, 0))
    return pl.pallas_call(
        up_kernel,
        grid=(1,),
        in_specs=[mix_spec] * 4
        + [
            pl.BlockSpec((rows, LANES), lambda i: (0, full // LANES - 1)),
            pl.BlockSpec((span * rank, width), lambda i: (0, 0)),
        ],
        out_specs=pl.BlockSpec((rows, width), lambda i: (0, 0)),
        out_shape=jax.ShapeDtypeStruct((rows, width), jnp.bfloat16),
        compiler_params=pltpu.CompilerParams(vmem_limit_bytes=VMEM // 4),
        cost_estimate=pl.CostEstimate(flops=2 * rows * up.size, bytes_accessed=2 * (up.size + rows * width), transcendentals=0),
        name="up_terms",
    )(*mixes, arrived, up.reshape(span * rank, width))


def finish_kernel(slots, own, from_below, from_above, terms, dest, out):
    drafts, rows, width = out.shape
    places = terms.shape[0]
    lane = lax.broadcasted_iota(jnp.int32, (rows, places), 1)
    where_to = dest[:, :1]
    for s in range(drafts):
        pick = jnp.where(lane == where_to + s * slots, 1.0, 0.0).astype(jnp.bfloat16)
        total = jnp.dot(pick, terms[...], preferred_element_type=jnp.float32)
        for ref in (own, from_below, from_above):
            total = total + ref[s * rows:(s + 1) * rows].astype(jnp.float32)
        out[s] = total.astype(jnp.bfloat16)


def finish(own, from_below, from_above, terms, dest, drafts, slots):
    rows = dest.shape[0]
    width = own.shape[1]
    return pl.pallas_call(
        functools.partial(finish_kernel, slots),
        out_shape=jax.ShapeDtypeStruct((drafts, rows, width), jnp.bfloat16),
        compiler_params=pltpu.CompilerParams(vmem_limit_bytes=VMEM // 4),
        cost_estimate=pl.CostEstimate(
            flops=2 * terms.size * rows * drafts, bytes_accessed=2 * terms.size, transcendentals=0
        ),
        name="finish",
    )(own, from_below, from_above, terms, dest)


def body(
    queries,
    draft_keys,
    draft_values,
    key_cache,
    value_cache,
    lengths,
    request_adapter,
    adapter_page_table,
    output_weight,
    adapter_down,
    adapter_up,
):
    drafts, rows, width = queries.shape
    owners = lax.axis_size("dp")
    parts = lax.axis_size("tensor")
    span, rank, _ = adapter_down.shape
    slots = rows // 8
    owner_rows = -(-drafts * slots // 8) * 8
    chips = parts // 2
    swap = [(i, i ^ 1) for i in range(parts)]
    shift = lambda k: [
        (2 * x + c, 2 * ((x + k) % chips) + c) for x in range(chips) for c in range(2)
    ]
    attn, payload, dest = attend(
        queries, draft_keys, draft_values, key_cache, value_cache, lengths, request_adapter,
        adapter_page_table, slots, owner_rows, owners, span,
    )
    arrived = lax.all_to_all(
        payload.reshape(owners, owner_rows, -1), "dp", 0, 0, tiled=True
    ).reshape(owners * owner_rows, -1)
    (sent,) = project(attn, output_weight, None, parts)
    other = lax.ppermute(sent, "tensor", swap)
    far_up, far_down, up, down, own = project(attn, output_weight, other, parts)
    far_up = lax.ppermute(far_up, "tensor", shift(1))
    far_down = lax.ppermute(far_down, "tensor", shift(-1))
    arrived, far_up, far_down = lax.optimization_barrier((arrived, far_up, far_down))
    mine = down_mix(arrived, adapter_down)
    pair = (mine + lax.ppermute(mine, "tensor", swap)).astype(jnp.bfloat16)
    mixes = [pair] + [lax.ppermute(pair, "tensor", shift(k)) for k in range(1, chips)]
    terms = up_terms(mixes, arrived, adapter_up)
    terms, far_up, far_down = lax.optimization_barrier((terms, far_up, far_down))
    up, down = merge(up, down, far_up, far_down)
    from_below = lax.ppermute(up, "tensor", shift(1))
    from_above = lax.ppermute(down, "tensor", shift(-1))
    terms = lax.all_to_all(
        terms.reshape(owners, owner_rows, -1), "dp", 0, 0, tiled=True
    ).reshape(owners * owner_rows, -1)
    return finish(own, from_below, from_above, terms, dest, drafts, slots)


def solution(mesh):
    placed = (
        P(None, "dp", "tensor"),
        P(None, "dp", "tensor"),
        P(None, "dp", "tensor"),
        P("dp", None, "tensor"),
        P("dp", None, "tensor"),
        P("dp"),
        P("dp"),
        P(),
        P("tensor", None),
        P("dp", None, "tensor"),
        P("dp", None, "tensor"),
    )
    return jax.shard_map(
        body, mesh=mesh, in_specs=placed, out_specs=P(None, "dp", "tensor"), check_vma=False
    )
```

```python
import functools, math
import jax, jax.numpy as jnp
from jax import lax
from jax.experimental import pallas as pl
from jax.experimental.pallas import tpu as pltpu
from jax.sharding import PartitionSpec as P

LANES = 128
STEP = 16
HALF = 8
AHEAD_COPIES = 3
PIECES = 8
IN_FLIGHT = 4
AHEAD = (2, 1, 3, 0)
VMEM = 63 * 1024 * 1024

def attend_kernel(
    slots, owner_rows, span, lengths, adapters_hbm, table_hbm, q_hbm, dk_hbm, dv_hbm, k_hbm, v_hbm,
    attn, payload, dest_out, adapters, table, q, dk, dv, k, v, scores, weights, small_sems, sems,
):
    drafts, count, width = q.shape
    cache = k.shape[1]
    heads = width // LANES
    rows = drafts * heads * HALF
    scale = math.log2(math.e) / math.sqrt(LANES)
    small = [
        pltpu.make_async_copy(a, b, small_sems.at[n])
        for n, (a, b) in enumerate(
            ((q_hbm, q), (dk_hbm, dk), (dv_hbm, dv), (adapters_hbm, adapters), (table_hbm, table))
        )
    ]

    steps = count // STEP
    flow = [(0, 0), (0, 1), (0, 2)] + [p for j in range(steps - 3) for p in ((1, j), (0, j + 3))] + [(1, j) for j in range(steps - 3, steps)]

    def fetch(at):
        n, j = flow[at]
        here = pl.ds(j * STEP, STEP)
        return pltpu.make_async_copy((k_hbm, v_hbm)[n].at[here], (k, v)[n].at[here], sems.at[n, j])

    def arrive(at):
        fetch(at).wait()
        if at + AHEAD_COPIES < len(flow):
            fetch(at + AHEAD_COPIES).start()

    for copy in small:
        copy.start()
    for at in range(AHEAD_COPIES):
        fetch(at).start()

    sub = lax.broadcasted_iota(jnp.int32, (rows, cache), 0) % HALF
    lane8 = lax.broadcasted_iota(jnp.int32, (HALF, cache), 1)
    sub8 = lax.broadcasted_iota(jnp.int32, (HALF, cache), 0)
    drow = lax.broadcasted_iota(jnp.int32, (rows, drafts * HALF), 0)
    dlane = lax.broadcasted_iota(jnp.int32, (rows, drafts * HALF), 1)
    fresh_ok = (drow % HALF == dlane % HALF) & (dlane // HALF <= drow // (heads * HALF))
    for copy in small[:3]:
        copy.wait()

    def places():
        for copy in small[3:]:
            copy.wait()
        pages = table.shape[1]
        a = lax.broadcasted_iota(jnp.int32, (count, count), 0)
        b = lax.broadcasted_iota(jnp.int32, (count, count), 1)
        eye = a == b
        to_col = lambda row: jnp.sum(jnp.where(eye, jnp.broadcast_to(row, (count, count)), 0.0), axis=1, keepdims=True)
        to_row = lambda col: jnp.sum(jnp.where(eye, jnp.broadcast_to(col, (count, count)), 0.0), axis=0, keepdims=True)
        acol = to_col(adapters[...].astype(jnp.float32)).astype(jnp.int32)
        hit = acol == lax.broadcasted_iota(jnp.int32, (count, pages), 1)
        page = jnp.sum(jnp.where(hit, jnp.broadcast_to(table[...].astype(jnp.float32), (count, pages)), 0.0), axis=1, keepdims=True)
        prow = to_row(page).astype(jnp.int32)
        pcol = page.astype(jnp.int32)
        orow, ocol = prow // span, pcol // span
        rank = jnp.sum(jnp.where((ocol == orow) & (a < b), 1.0, 0.0), axis=0, keepdims=True).astype(jnp.int32)
        rank_col = jnp.sum(jnp.where((ocol == orow) & (b < a), 1.0, 0.0), axis=1, keepdims=True).astype(jnp.int32)
        dest_out[...] = jnp.broadcast_to(ocol * owner_rows + rank_col, dest_out.shape)
        dest = orow * owner_rows + rank
        local = jnp.broadcast_to((pcol - ocol * span).astype(jnp.float32), (count, LANES)).astype(jnp.bfloat16)
        return dest, local

    def score(j, carry):
        base = j * STEP
        here = pl.ds(base, STEP)
        qf = q[:, here].astype(jnp.float32)
        dkf = dk[:, here].astype(jnp.float32)
        arrive(flow.index((0, j)))
        for h in range(STEP // HALF):
            at = slice(h * HALF, (h + 1) * HALF)
            qb = jnp.concatenate([qf[s, at, g * LANES:(g + 1) * LANES] for s in range(drafts) for g in range(heads)], axis=0).astype(jnp.bfloat16)
            kb = jnp.concatenate([dkf[t, at] for t in range(drafts)], axis=0).astype(jnp.bfloat16)
            part = None
            limit = jnp.zeros((HALF, cache), jnp.int32)
            for r in range(HALF):
                one = lax.dot_general(qb, k[base + h * HALF + r], (((1,), (1,)), ((), ())), preferred_element_type=jnp.float32)
                part = one if r == 0 else jnp.where(sub == r, one, part)
                limit = jnp.where(sub8 == r, lengths[base + h * HALF + r], limit)
            seen = jnp.concatenate([(lane8 < limit).astype(jnp.int32)] * (drafts * heads), axis=0) > 0
            fresh = lax.dot_general(qb, kb, (((1,), (1,)), ((), ())), preferred_element_type=jnp.float32)
            scores[j, h, :, :cache] = jnp.where(seen, part, -1e30)
            scores[j, h, :, cache:cache + drafts * HALF] = jnp.where(fresh_ok, fresh, -1e30)
        return carry

    def soften(j, carry):
        for h in range(STEP // HALF):
            part = scores[j, h, :, :cache]
            fresh = scores[j, h, :, cache:cache + drafts * HALF]
            top = jnp.maximum(jnp.max(part, axis=1, keepdims=True), jnp.max(fresh, axis=1, keepdims=True))
            e = jnp.exp2((part - top) * scale)
            ef = jnp.exp2((fresh - top) * scale)
            inv = 1.0 / (jnp.sum(e, axis=1, keepdims=True) + jnp.sum(ef, axis=1, keepdims=True))
            weights[j, h, :, :cache] = (e * inv).astype(jnp.bfloat16)
            weights[j, h, :, cache:cache + drafts * HALF] = (ef * inv).astype(jnp.bfloat16)
        return carry

    keep = [jnp.where(sub == r, 1.0, 0.0).astype(jnp.bfloat16) for r in range(HALF)]

    def mix(j, carry):
        base = j * STEP
        here = pl.ds(base, STEP)
        dvf = dv[:, here].astype(jnp.float32)
        arrive(flow.index((1, j)))
        outs = []
        for h in range(STEP // HALF):
            at = slice(h * HALF, (h + 1) * HALF)
            vb = jnp.concatenate([dvf[t, at] for t in range(drafts)], axis=0).astype(jnp.bfloat16)
            w = weights[j, h, :, :cache]
            wf = weights[j, h, :, cache:cache + drafts * HALF]
            wide = jnp.concatenate([w * keep[r] for r in range(HALF)], axis=1)
            vals = v[pl.ds(base + h * HALF, HALF)].reshape(HALF * cache, LANES)
            mixed = jnp.dot(wide, vals, preferred_element_type=jnp.float32)
            mixed = mixed + jnp.dot(wf, vb, preferred_element_type=jnp.float32)
            outs.append(mixed)
        for s in range(drafts):
            for g in range(heads):
                at = (s * heads + g) * HALF
                piece = jnp.concatenate([o[at:at + HALF] for o in outs], axis=0).astype(jnp.bfloat16)
                attn[s, here, g * LANES:(g + 1) * LANES] = piece
        return carry

    for j in range(steps + 2):
        if j < steps:
            score(j, 0)
        if j == 1:
            dest, local = places()
        if 1 <= j <= steps:
            soften(j - 1, 0)
        if j >= 2:
            mix(j - 2, 0)

    place = lax.broadcasted_iota(jnp.int32, (payload.shape[0], count), 0)
    acc = None
    for s in range(drafts):
        pick = jnp.where(place == dest + s * slots, 1.0, 0.0).astype(jnp.bfloat16)
        part = jnp.dot(pick, jnp.concatenate([attn[s], local], axis=1), preferred_element_type=jnp.float32)
        acc = part if acc is None else acc + part
    payload[...] = acc.astype(jnp.bfloat16)


def attend(queries, draft_keys, draft_values, key_cache, value_cache, lengths, request_adapter, table, slots, owner_rows, owners, span):
    drafts, rows, width = queries.shape
    cache = key_cache.shape[1]
    vmem = pl.BlockSpec(memory_space=pltpu.VMEM)
    hbm = pl.BlockSpec(memory_space=pltpu.HBM)
    return pl.pallas_call(
        functools.partial(attend_kernel, slots, owner_rows, span),
        in_specs=[pl.BlockSpec(memory_space=pltpu.SMEM)] + [hbm] * 7,
        out_specs=[vmem] * 3,
        out_shape=[
            jax.ShapeDtypeStruct((drafts, rows, width), jnp.bfloat16),
            jax.ShapeDtypeStruct((owners * owner_rows, width + LANES), jnp.bfloat16),
            jax.ShapeDtypeStruct((rows, LANES), jnp.int32),
        ],
        scratch_shapes=[
            pltpu.VMEM((1, rows), jnp.int32),
            pltpu.VMEM((1, table.shape[0]), jnp.int32),
            pltpu.VMEM(queries.shape, jnp.bfloat16),
            pltpu.VMEM(draft_keys.shape, jnp.bfloat16),
            pltpu.VMEM(draft_values.shape, jnp.bfloat16),
            pltpu.VMEM(key_cache.shape, jnp.bfloat16),
            pltpu.VMEM(value_cache.shape, jnp.bfloat16),
            pltpu.VMEM((rows // STEP, STEP // HALF, drafts * width // LANES * HALF, cache + LANES), jnp.float32),
            pltpu.VMEM((rows // STEP, STEP // HALF, drafts * width // LANES * HALF, cache + LANES), jnp.bfloat16),
            pltpu.SemaphoreType.DMA((5,)),
            pltpu.SemaphoreType.DMA((2, rows // STEP)),
        ],
        compiler_params=pltpu.CompilerParams(vmem_limit_bytes=VMEM),
        cost_estimate=pl.CostEstimate(
            flops=8 * queries.size * cache, bytes_accessed=4 * key_cache.size, transcendentals=0
        ),
        name="attend",
    )(lengths, request_adapter.reshape(1, rows), table.reshape(1, -1), queries, draft_keys, draft_values, key_cache, value_cache)


def project_kernel(first, attn, attn_other, weight, weight_other, *refs):
    outs, (flat, held, done, sems, in_sems, out_sems) = refs[:-6], refs[-6:]
    _, half, width = flat.shape
    half = half // 2
    place = lax.axis_index("tensor")
    chips = lax.axis_size("tensor") // 2
    blocks, sources, _, part = held.shape
    flow = [(j, n) for j in range(blocks) for n in range(sources)]
    piece = width // PIECES

    def fetch(at, s=None):
        j, n = flow[at]
        block = (place // 2 + AHEAD[first + j]) % chips * 2 + place % 2
        here = pl.ds(pl.multiple_of(block * part, part), part)
        w, to = (weight, weight_other)[n], held.at[j, n]
        if s is None:
            return pltpu.make_async_copy(w.at[:, here], to, sems.at[j, n])
        down = pl.ds(s * piece, piece)
        return pltpu.make_async_copy(w.at[down, here], to.at[down], sems.at[j, n])

    def begin(at):
        for s in range(PIECES):
            fetch(at, s).start()

    ins = [pltpu.make_async_copy(a, flat.at[n], in_sems.at[n]) for n, a in enumerate((attn, attn_other))]
    for copy in ins:
        copy.start()
    for at in range(min(IN_FLIGHT, len(flow))):
        begin(at)
    for copy in ins:
        copy.wait()
    stores = []
    for j in range(blocks):
        total = None
        for n in range(sources):
            at = j * sources + n
            fetch(at).wait()
            if at + IN_FLIGHT < len(flow):
                begin(at + IN_FLIGHT)
            part_sum = jnp.dot(flat[n], held[j, n], preferred_element_type=jnp.float32)
            total = part_sum if total is None else total + part_sum
        done[j] = total.astype(jnp.bfloat16)
        for n in range(2):
            at = 2 * j + n
            stores.append(pltpu.make_async_copy(done.at[j, pl.ds(n * half, half)], outs[at], out_sems.at[at]))
            stores[-1].start()
    for store in stores:
        store.wait()


def project(attn, attn_other, weight, weight_other, parts, first, blocks):
    rows, width = attn.shape
    part = weight.shape[1] // parts
    hbm = pl.BlockSpec(memory_space=pltpu.HBM)
    half = jax.ShapeDtypeStruct((rows // 2, part), jnp.bfloat16)
    return pl.pallas_call(
        functools.partial(project_kernel, first),
        in_specs=[hbm] * 4,
        out_specs=[hbm] * (2 * blocks),
        out_shape=[half] * (2 * blocks),
        scratch_shapes=[
            pltpu.VMEM((2, rows, width), jnp.bfloat16),
            pltpu.VMEM((blocks, 2, width, part), jnp.bfloat16),
            pltpu.VMEM((blocks, rows, part), jnp.bfloat16),
            pltpu.SemaphoreType.DMA((blocks, 2)),
            pltpu.SemaphoreType.DMA((2,)),
            pltpu.SemaphoreType.DMA((2 * blocks,)),
        ],
        compiler_params=pltpu.CompilerParams(vmem_limit_bytes=VMEM),
        cost_estimate=pl.CostEstimate(
            flops=4 * rows * width * part * blocks,
            bytes_accessed=4 * width * part * blocks,
            transcendentals=0,
        ),
        name="project",
    )(attn, attn_other, weight, weight_other)


def merge_kernel(up, down, far_up, far_down, up_out, down_out):
    for a, b, out in ((up, far_up, up_out), (down, far_down, down_out)):
        out[...] = (a[...].astype(jnp.float32) + b[...].astype(jnp.float32)).astype(jnp.bfloat16)


def merge(up, down, far_up, far_down):
    shape = jax.ShapeDtypeStruct(up.shape, up.dtype)
    return pl.pallas_call(
        merge_kernel,
        out_shape=[shape, shape],
        compiler_params=pltpu.CompilerParams(vmem_limit_bytes=VMEM // 4),
        cost_estimate=pl.CostEstimate(flops=0, bytes_accessed=12 * up.size, transcendentals=0),
        name="merge",
    )(up, down, far_up, far_down)


def down_kernel(arrived, down, mix):
    width = down.shape[1]
    span = down.shape[0] // mix.shape[0]
    product = lax.dot_general(
        down[...], arrived[:, :width], (((1,), (1,)), ((), ())), preferred_element_type=jnp.float32
    )
    ones = jnp.ones((8, LANES), jnp.bfloat16)
    page = lax.dot_general(
        ones, arrived[:, width:], (((1,), (1,)), ((), ())), preferred_element_type=jnp.float32
    )[:1] * (1.0 / LANES)
    rank = mix.shape[0]
    total = jnp.zeros(mix.shape, jnp.float32)
    for p in range(span):
        total = total + jnp.where(page == float(p), product[p * rank:(p + 1) * rank], 0.0)
    mix[...] = total


def down_mix(arrived, down):
    rows = arrived.shape[0]
    span, rank, width = down.shape
    return pl.pallas_call(
        down_kernel,
        out_shape=jax.ShapeDtypeStruct((rank, rows), jnp.float32),
        compiler_params=pltpu.CompilerParams(vmem_limit_bytes=VMEM // 4),
        cost_estimate=pl.CostEstimate(flops=2 * rows * down.size, bytes_accessed=2 * (arrived.size + down.size), transcendentals=0),
        name="down_mix",
    )(arrived, down.reshape(span * rank, width))


def up_kernel(mine, one, two, three, arrived, up, out):
    rank = mine.shape[0]
    spread_width = up.shape[0]
    mix = (
        mine[...].astype(jnp.float32)
        + one[...].astype(jnp.float32)
        + two[...].astype(jnp.float32)
        + three[...].astype(jnp.float32)
    ).astype(jnp.bfloat16)
    a = lax.broadcasted_iota(jnp.int32, (rank, spread_width), 0)
    b = lax.broadcasted_iota(jnp.int32, (rank, spread_width), 1)
    repeat = jnp.where(b % rank == a, 1.0, 0.0).astype(jnp.bfloat16)
    spread = lax.dot_general(
        mix, repeat, (((0,), (0,)), ((), ())), preferred_element_type=jnp.float32
    )
    meta = arrived[...].astype(jnp.float32)
    pieces = []
    for j in range(spread_width // LANES):
        lane = lax.broadcasted_iota(jnp.int32, meta.shape, 1) + j * LANES
        same = meta == (lane // rank).astype(jnp.float32)
        pieces.append(jnp.where(same, spread[:, j * LANES:(j + 1) * LANES], 0.0).astype(jnp.bfloat16))
    out[...] = jnp.dot(
        jnp.concatenate(pieces, axis=1), up[...], preferred_element_type=jnp.float32
    ).astype(jnp.bfloat16)


def up_terms(mixes, arrived, up):
    rows, full = arrived.shape
    span, rank, width = up.shape
    mix_spec = pl.BlockSpec((rank, rows), lambda i: (0, 0))
    return pl.pallas_call(
        up_kernel,
        grid=(1,),
        in_specs=[mix_spec] * 4
        + [
            pl.BlockSpec((rows, LANES), lambda i: (0, full // LANES - 1)),
            pl.BlockSpec((span * rank, width), lambda i: (0, 0)),
        ],
        out_specs=pl.BlockSpec((rows, width), lambda i: (0, 0)),
        out_shape=jax.ShapeDtypeStruct((rows, width), jnp.bfloat16),
        compiler_params=pltpu.CompilerParams(vmem_limit_bytes=VMEM // 4),
        cost_estimate=pl.CostEstimate(flops=2 * rows * up.size, bytes_accessed=2 * (up.size + rows * width), transcendentals=0),
        name="up_terms",
    )(*mixes, arrived, up.reshape(span * rank, width))


def finish_kernel(slots, *refs):
    halves, (terms, dest, out) = refs[:6], refs[6:]
    drafts, rows, width = out.shape
    places = terms.shape[0]
    lane = lax.broadcasted_iota(jnp.int32, (rows, places), 1)
    where_to = dest[:, :1]
    total = []
    for n in range(2):
        a, b, c = halves[n::2]
        total.append(a[...].astype(jnp.float32) + b[...].astype(jnp.float32) + c[...].astype(jnp.float32))
    total = jnp.concatenate(total, axis=0)
    for s in range(drafts):
        pick = jnp.where(lane == where_to + s * slots, 1.0, 0.0).astype(jnp.bfloat16)
        term = jnp.dot(pick, terms[...], preferred_element_type=jnp.float32)
        out[s] = (total[s * rows:(s + 1) * rows] + term).astype(jnp.bfloat16)


def finish(halves, terms, dest, drafts, slots):
    rows = dest.shape[0]
    width = terms.shape[1]
    return pl.pallas_call(
        functools.partial(finish_kernel, slots),
        out_shape=jax.ShapeDtypeStruct((drafts, rows, width), jnp.bfloat16),
        compiler_params=pltpu.CompilerParams(vmem_limit_bytes=VMEM // 4),
        cost_estimate=pl.CostEstimate(
            flops=2 * terms.size * rows * drafts, bytes_accessed=2 * terms.size, transcendentals=0
        ),
        name="finish",
    )(*halves, terms, dest)


def body(
    queries,
    draft_keys,
    draft_values,
    key_cache,
    value_cache,
    lengths,
    request_adapter,
    adapter_page_table,
    output_weight,
    adapter_down,
    adapter_up,
):
    drafts, rows, width = queries.shape
    owners = lax.axis_size("dp")
    parts = lax.axis_size("tensor")
    span, rank, _ = adapter_down.shape
    slots = rows // 8
    owner_rows = -(-drafts * slots // 8) * 8
    chips = parts // 2
    swap = [(i, i ^ 1) for i in range(parts)]
    shift = lambda k: [
        (2 * x + c, 2 * ((x + k) % chips) + c) for x in range(chips) for c in range(2)
    ]
    weight_other = lax.ppermute(output_weight, "tensor", swap)
    attn, payload, dest = attend(
        queries, draft_keys, draft_values, key_cache, value_cache, lengths, request_adapter,
        adapter_page_table, slots, owner_rows, owners, span,
    )
    arrived = lax.all_to_all(
        payload.reshape(owners, owner_rows, -1), "dp", 0, 0, tiled=True
    ).reshape(owners * owner_rows, -1)
    attn = attn.reshape(drafts * rows, width)
    attn_other = lax.ppermute(attn, "tensor", swap)
    blocks = project(attn, attn_other, output_weight, weight_other, parts, 0, chips)
    far_up, far_down, up, near_up, near_down, down, own_top, own_bottom = blocks
    far_up = lax.ppermute(far_up, "tensor", shift(1))
    far_down = lax.ppermute(far_down, "tensor", shift(-1))
    mine = down_mix(arrived, adapter_down)
    mine, far_up, far_down = lax.optimization_barrier((mine, far_up, far_down))
    pair = (mine + lax.ppermute(mine, "tensor", swap)).astype(jnp.bfloat16)
    mixes = [pair] + [lax.ppermute(pair, "tensor", shift(k)) for k in range(1, chips)]
    terms = up_terms(mixes, arrived, adapter_up)
    terms, up, down, near_up, near_down = lax.optimization_barrier(
        (terms, up, down, near_up, near_down)
    )
    from_below = lax.ppermute(near_up, "tensor", shift(1))
    from_above = lax.ppermute(near_down, "tensor", shift(-1))
    up, down = merge(up, down, far_up, far_down)
    up = lax.ppermute(up, "tensor", shift(1))
    down = lax.ppermute(down, "tensor", shift(-1))
    terms = lax.all_to_all(
        terms.reshape(owners, owner_rows, -1), "dp", 0, 0, tiled=True
    ).reshape(owners * owner_rows, -1)
    halves = (own_top, own_bottom, up, from_below, from_above, down)
    return finish(halves, terms, dest, drafts, slots)


def solution(mesh):
    placed = (
        P(None, "dp", "tensor"),
        P(None, "dp", "tensor"),
        P(None, "dp", "tensor"),
        P("dp", None, "tensor"),
        P("dp", None, "tensor"),
        P("dp"),
        P("dp"),
        P(),
        P("tensor", None),
        P("dp", None, "tensor"),
        P("dp", None, "tensor"),
    )
    return jax.shard_map(
        body, mesh=mesh, in_specs=placed, out_specs=P(None, "dp", "tensor"), check_vma=False
    )
```

```python
import functools, math
import jax, jax.numpy as jnp
from jax import lax
from jax.experimental import pallas as pl
from jax.experimental.pallas import tpu as pltpu
from jax.sharding import PartitionSpec as P

LANES = 128
STEP = 16
HALF = 8
AHEAD_COPIES = 3
PIECES = 8
IN_FLIGHT = 4
AHEAD = (2, 1, 3, 0)
VMEM = 63 * 1024 * 1024

def attend_kernel(
    slots, owner_rows, span, lengths, adapters_hbm, table_hbm, q_hbm, dk_hbm, dv_hbm, k_hbm, v_hbm,
    attn, payload, dest_out, adapters, table, q, dk, dv, k, v, scores, weights, small_sems, sems,
):
    drafts, count, width = q.shape
    cache = k.shape[1]
    heads = width // LANES
    rows = drafts * heads * HALF
    scale = math.log2(math.e) / math.sqrt(LANES)
    small = [
        pltpu.make_async_copy(a, b, small_sems.at[n])
        for n, (a, b) in enumerate(
            ((q_hbm, q), (dk_hbm, dk), (dv_hbm, dv), (adapters_hbm, adapters), (table_hbm, table))
        )
    ]

    steps = count // STEP
    flow = [(0, 0), (0, 1), (0, 2)] + [p for j in range(steps - 3) for p in ((1, j), (0, j + 3))] + [(1, j) for j in range(steps - 3, steps)]

    def fetch(at):
        n, j = flow[at]
        here = pl.ds(j * STEP, STEP)
        return pltpu.make_async_copy((k_hbm, v_hbm)[n].at[here], (k, v)[n].at[here], sems.at[n, j])

    def arrive(at):
        fetch(at).wait()
        if at + AHEAD_COPIES < len(flow):
            fetch(at + AHEAD_COPIES).start()

    for copy in small:
        copy.start()
    for at in range(AHEAD_COPIES):
        fetch(at).start()

    sub = lax.broadcasted_iota(jnp.int32, (rows, cache), 0) % HALF
    lane8 = lax.broadcasted_iota(jnp.int32, (HALF, cache), 1)
    sub8 = lax.broadcasted_iota(jnp.int32, (HALF, cache), 0)
    drow = lax.broadcasted_iota(jnp.int32, (rows, drafts * HALF), 0)
    dlane = lax.broadcasted_iota(jnp.int32, (rows, drafts * HALF), 1)
    fresh_ok = (drow % HALF == dlane % HALF) & (dlane // HALF <= drow // (heads * HALF))
    for copy in small[:3]:
        copy.wait()

    def places():
        for copy in small[3:]:
            copy.wait()
        pages = table.shape[1]
        a = lax.broadcasted_iota(jnp.int32, (count, count), 0)
        b = lax.broadcasted_iota(jnp.int32, (count, count), 1)
        eye = a == b
        to_col = lambda row: jnp.sum(jnp.where(eye, jnp.broadcast_to(row, (count, count)), 0.0), axis=1, keepdims=True)
        to_row = lambda col: jnp.sum(jnp.where(eye, jnp.broadcast_to(col, (count, count)), 0.0), axis=0, keepdims=True)
        acol = to_col(adapters[...].astype(jnp.float32)).astype(jnp.int32)
        hit = acol == lax.broadcasted_iota(jnp.int32, (count, pages), 1)
        page = jnp.sum(jnp.where(hit, jnp.broadcast_to(table[...].astype(jnp.float32), (count, pages)), 0.0), axis=1, keepdims=True)
        prow = to_row(page).astype(jnp.int32)
        pcol = page.astype(jnp.int32)
        orow, ocol = prow // span, pcol // span
        rank = jnp.sum(jnp.where((ocol == orow) & (a < b), 1.0, 0.0), axis=0, keepdims=True).astype(jnp.int32)
        rank_col = jnp.sum(jnp.where((ocol == orow) & (b < a), 1.0, 0.0), axis=1, keepdims=True).astype(jnp.int32)
        dest_out[...] = jnp.broadcast_to(ocol * owner_rows + rank_col, dest_out.shape)
        dest = orow * owner_rows + rank
        local = jnp.broadcast_to((pcol - ocol * span).astype(jnp.float32), (count, LANES)).astype(jnp.bfloat16)
        return dest, local

    def score(j, carry):
        base = j * STEP
        here = pl.ds(base, STEP)
        qf = q[:, here].astype(jnp.float32)
        dkf = dk[:, here].astype(jnp.float32)
        arrive(flow.index((0, j)))
        for h in range(STEP // HALF):
            at = slice(h * HALF, (h + 1) * HALF)
            qb = jnp.concatenate([qf[s, at, g * LANES:(g + 1) * LANES] for s in range(drafts) for g in range(heads)], axis=0).astype(jnp.bfloat16)
            kb = jnp.concatenate([dkf[t, at] for t in range(drafts)], axis=0).astype(jnp.bfloat16)
            part = None
            limit = jnp.zeros((HALF, cache), jnp.int32)
            for r in range(HALF):
                one = lax.dot_general(qb, k[base + h * HALF + r], (((1,), (1,)), ((), ())), preferred_element_type=jnp.float32)
                part = one if r == 0 else jnp.where(sub == r, one, part)
                limit = jnp.where(sub8 == r, lengths[base + h * HALF + r], limit)
            seen = jnp.concatenate([(lane8 < limit).astype(jnp.int32)] * (drafts * heads), axis=0) > 0
            fresh = lax.dot_general(qb, kb, (((1,), (1,)), ((), ())), preferred_element_type=jnp.float32)
            scores[j, h, :, :cache] = jnp.where(seen, part, -1e30)
            scores[j, h, :, cache:cache + drafts * HALF] = jnp.where(fresh_ok, fresh, -1e30)
        return carry

    def soften(j, carry):
        for h in range(STEP // HALF):
            part = scores[j, h, :, :cache]
            fresh = scores[j, h, :, cache:cache + drafts * HALF]
            top = jnp.maximum(jnp.max(part, axis=1, keepdims=True), jnp.max(fresh, axis=1, keepdims=True))
            e = jnp.exp2((part - top) * scale)
            ef = jnp.exp2((fresh - top) * scale)
            inv = 1.0 / (jnp.sum(e, axis=1, keepdims=True) + jnp.sum(ef, axis=1, keepdims=True))
            weights[j, h, :, :cache] = (e * inv).astype(jnp.bfloat16)
            weights[j, h, :, cache:cache + drafts * HALF] = (ef * inv).astype(jnp.bfloat16)
        return carry

    keep = [jnp.where(sub == r, 1.0, 0.0).astype(jnp.bfloat16) for r in range(HALF)]

    def mix(j, carry):
        base = j * STEP
        here = pl.ds(base, STEP)
        dvf = dv[:, here].astype(jnp.float32)
        arrive(flow.index((1, j)))
        outs = []
        for h in range(STEP // HALF):
            at = slice(h * HALF, (h + 1) * HALF)
            vb = jnp.concatenate([dvf[t, at] for t in range(drafts)], axis=0).astype(jnp.bfloat16)
            w = weights[j, h, :, :cache]
            wf = weights[j, h, :, cache:cache + drafts * HALF]
            wide = jnp.concatenate([w * keep[r] for r in range(HALF)], axis=1)
            vals = v[pl.ds(base + h * HALF, HALF)].reshape(HALF * cache, LANES)
            mixed = jnp.dot(wide, vals, preferred_element_type=jnp.float32)
            mixed = mixed + jnp.dot(wf, vb, preferred_element_type=jnp.float32)
            outs.append(mixed)
        for s in range(drafts):
            for g in range(heads):
                at = (s * heads + g) * HALF
                piece = jnp.concatenate([o[at:at + HALF] for o in outs], axis=0).astype(jnp.bfloat16)
                attn[s, here, g * LANES:(g + 1) * LANES] = piece
        return carry

    for j in range(steps + 2):
        if j < steps:
            score(j, 0)
        if j == 1:
            dest, local = places()
        if 1 <= j <= steps:
            soften(j - 1, 0)
        if j >= 2:
            mix(j - 2, 0)

    place = lax.broadcasted_iota(jnp.int32, (payload.shape[0], count), 0)
    acc = None
    for s in range(drafts):
        pick = jnp.where(place == dest + s * slots, 1.0, 0.0).astype(jnp.bfloat16)
        part = jnp.dot(pick, jnp.concatenate([attn[s], local], axis=1), preferred_element_type=jnp.float32)
        acc = part if acc is None else acc + part
    payload[...] = acc.astype(jnp.bfloat16)


def attend(queries, draft_keys, draft_values, key_cache, value_cache, lengths, request_adapter, table, slots, owner_rows, owners, span):
    drafts, rows, width = queries.shape
    cache = key_cache.shape[1]
    vmem = pl.BlockSpec(memory_space=pltpu.VMEM)
    hbm = pl.BlockSpec(memory_space=pltpu.HBM)
    return pl.pallas_call(
        functools.partial(attend_kernel, slots, owner_rows, span),
        in_specs=[pl.BlockSpec(memory_space=pltpu.SMEM)] + [hbm] * 7,
        out_specs=[vmem] * 3,
        out_shape=[
            jax.ShapeDtypeStruct((drafts, rows, width), jnp.bfloat16),
            jax.ShapeDtypeStruct((owners * owner_rows, width + LANES), jnp.bfloat16),
            jax.ShapeDtypeStruct((rows, LANES), jnp.int32),
        ],
        scratch_shapes=[
            pltpu.VMEM((1, rows), jnp.int32),
            pltpu.VMEM((1, table.shape[0]), jnp.int32),
            pltpu.VMEM(queries.shape, jnp.bfloat16),
            pltpu.VMEM(draft_keys.shape, jnp.bfloat16),
            pltpu.VMEM(draft_values.shape, jnp.bfloat16),
            pltpu.VMEM(key_cache.shape, jnp.bfloat16),
            pltpu.VMEM(value_cache.shape, jnp.bfloat16),
            pltpu.VMEM((rows // STEP, STEP // HALF, drafts * width // LANES * HALF, cache + LANES), jnp.float32),
            pltpu.VMEM((rows // STEP, STEP // HALF, drafts * width // LANES * HALF, cache + LANES), jnp.bfloat16),
            pltpu.SemaphoreType.DMA((5,)),
            pltpu.SemaphoreType.DMA((2, rows // STEP)),
        ],
        compiler_params=pltpu.CompilerParams(vmem_limit_bytes=VMEM),
        cost_estimate=pl.CostEstimate(
            flops=8 * queries.size * cache, bytes_accessed=4 * key_cache.size, transcendentals=0
        ),
        name="attend",
    )(lengths, request_adapter.reshape(1, rows), table.reshape(1, -1), queries, draft_keys, draft_values, key_cache, value_cache)


def project_kernel(first, cuts, attn, attn_other, weight, weight_other, *refs):
    outs, (flat, held, done, sems, in_sems, out_sems) = refs[:-6], refs[-6:]
    _, rows, width = flat.shape
    place = lax.axis_index("tensor")
    chips = lax.axis_size("tensor") // 2
    blocks, sources, _, part = held.shape
    flow = [(j, n) for j in range(blocks) for n in range(sources)]
    piece = width // PIECES

    def fetch(at, s=None):
        j, n = flow[at]
        block = (place // 2 + AHEAD[first + j]) % chips * 2 + place % 2
        here = pl.ds(pl.multiple_of(block * part, part), part)
        w, to = (weight, weight_other)[n], held.at[j, n]
        if s is None:
            return pltpu.make_async_copy(w.at[:, here], to, sems.at[j, n])
        down = pl.ds(s * piece, piece)
        return pltpu.make_async_copy(w.at[down, here], to.at[down], sems.at[j, n])

    def begin(at):
        for s in range(PIECES):
            fetch(at, s).start()

    ins = [pltpu.make_async_copy(a, flat.at[n], in_sems.at[n]) for n, a in enumerate((attn, attn_other))]
    for copy in ins:
        copy.start()
    for at in range(min(IN_FLIGHT, len(flow))):
        begin(at)
    for copy in ins:
        copy.wait()
    stores = []
    for j in range(blocks):
        total = None
        for n in range(sources):
            at = j * sources + n
            fetch(at).wait()
            if at + IN_FLIGHT < len(flow):
                begin(at + IN_FLIGHT)
            part_sum = jnp.dot(flat[n], held[j, n], preferred_element_type=jnp.float32)
            total = part_sum if total is None else total + part_sum
        done[j] = total.astype(jnp.bfloat16)
        for n in range(cuts):
            at = cuts * j + n
            here = pl.ds(n * (rows // cuts), rows // cuts)
            stores.append(pltpu.make_async_copy(done.at[j, here], outs[at], out_sems.at[at]))
            stores[-1].start()
    for store in stores:
        store.wait()


def project(attn, attn_other, weight, weight_other, parts, first, blocks, cuts=2):
    rows, width = attn.shape
    part = weight.shape[1] // parts
    hbm = pl.BlockSpec(memory_space=pltpu.HBM)
    piece = jax.ShapeDtypeStruct((rows // cuts, part), jnp.bfloat16)
    return pl.pallas_call(
        functools.partial(project_kernel, first, cuts),
        in_specs=[hbm] * 4,
        out_specs=[hbm] * (cuts * blocks),
        out_shape=[piece] * (cuts * blocks),
        scratch_shapes=[
            pltpu.VMEM((2, rows, width), jnp.bfloat16),
            pltpu.VMEM((blocks, 2, width, part), jnp.bfloat16),
            pltpu.VMEM((blocks, rows, part), jnp.bfloat16),
            pltpu.SemaphoreType.DMA((blocks, 2)),
            pltpu.SemaphoreType.DMA((2,)),
            pltpu.SemaphoreType.DMA((cuts * blocks,)),
        ],
        compiler_params=pltpu.CompilerParams(vmem_limit_bytes=VMEM * 8 // 9),
        cost_estimate=pl.CostEstimate(
            flops=16 * rows * width * part * blocks,
            bytes_accessed=16 * width * part * blocks,
            transcendentals=0,
        ),
        name="project",
    )(attn, attn_other, weight, weight_other)


def merge_kernel(up, down, far_up, far_down, up_out, down_out):
    for a, b, out in ((up, far_up, up_out), (down, far_down, down_out)):
        out[...] = (a[...].astype(jnp.float32) + b[...].astype(jnp.float32)).astype(jnp.bfloat16)


def merge(up, down, far_up, far_down):
    shape = jax.ShapeDtypeStruct(up.shape, up.dtype)
    return pl.pallas_call(
        merge_kernel,
        out_shape=[shape, shape],
        compiler_params=pltpu.CompilerParams(vmem_limit_bytes=VMEM // 4),
        cost_estimate=pl.CostEstimate(flops=0, bytes_accessed=12 * up.size, transcendentals=0),
        name="merge",
    )(up, down, far_up, far_down)


def down_kernel(arrived, down, mix):
    width = down.shape[1]
    span = down.shape[0] // mix.shape[0]
    product = lax.dot_general(
        down[...], arrived[:, :width], (((1,), (1,)), ((), ())), preferred_element_type=jnp.float32
    )
    ones = jnp.ones((8, LANES), jnp.bfloat16)
    page = lax.dot_general(
        ones, arrived[:, width:], (((1,), (1,)), ((), ())), preferred_element_type=jnp.float32
    )[:1] * (1.0 / LANES)
    rank = mix.shape[0]
    total = jnp.zeros(mix.shape, jnp.float32)
    for p in range(span):
        total = total + jnp.where(page == float(p), product[p * rank:(p + 1) * rank], 0.0)
    mix[...] = total


def down_mix(arrived, down):
    rows = arrived.shape[0]
    span, rank, width = down.shape
    return pl.pallas_call(
        down_kernel,
        out_shape=jax.ShapeDtypeStruct((rank, rows), jnp.float32),
        compiler_params=pltpu.CompilerParams(vmem_limit_bytes=VMEM // 4),
        cost_estimate=pl.CostEstimate(flops=2 * rows * down.size, bytes_accessed=2 * (arrived.size + down.size), transcendentals=0),
        name="down_mix",
    )(arrived, down.reshape(span * rank, width))


def up_kernel(mine, one, two, three, arrived, up, out):
    rank = mine.shape[0]
    spread_width = up.shape[0]
    mix = (
        mine[...].astype(jnp.float32)
        + one[...].astype(jnp.float32)
        + two[...].astype(jnp.float32)
        + three[...].astype(jnp.float32)
    ).astype(jnp.bfloat16)
    a = lax.broadcasted_iota(jnp.int32, (rank, spread_width), 0)
    b = lax.broadcasted_iota(jnp.int32, (rank, spread_width), 1)
    repeat = jnp.where(b % rank == a, 1.0, 0.0).astype(jnp.bfloat16)
    spread = lax.dot_general(
        mix, repeat, (((0,), (0,)), ((), ())), preferred_element_type=jnp.float32
    )
    meta = arrived[...].astype(jnp.float32)
    pieces = []
    for j in range(spread_width // LANES):
        lane = lax.broadcasted_iota(jnp.int32, meta.shape, 1) + j * LANES
        same = meta == (lane // rank).astype(jnp.float32)
        pieces.append(jnp.where(same, spread[:, j * LANES:(j + 1) * LANES], 0.0).astype(jnp.bfloat16))
    out[...] = jnp.dot(
        jnp.concatenate(pieces, axis=1), up[...], preferred_element_type=jnp.float32
    ).astype(jnp.bfloat16)


def up_terms(mixes, arrived, up):
    rows, full = arrived.shape
    span, rank, width = up.shape
    mix_spec = pl.BlockSpec((rank, rows), lambda i: (0, 0))
    return pl.pallas_call(
        up_kernel,
        grid=(1,),
        in_specs=[mix_spec] * 4
        + [
            pl.BlockSpec((rows, LANES), lambda i: (0, full // LANES - 1)),
            pl.BlockSpec((span * rank, width), lambda i: (0, 0)),
        ],
        out_specs=pl.BlockSpec((rows, width), lambda i: (0, 0)),
        out_shape=jax.ShapeDtypeStruct((rows, width), jnp.bfloat16),
        compiler_params=pltpu.CompilerParams(vmem_limit_bytes=VMEM // 4),
        cost_estimate=pl.CostEstimate(flops=2 * rows * up.size, bytes_accessed=2 * (up.size + rows * width), transcendentals=0),
        name="up_terms",
    )(*mixes, arrived, up.reshape(span * rank, width))


def gather_kernel(own, *refs):
    parts, out = refs[:4], refs[4]
    half = parts[0].shape[0]
    for n in range(2):
        here = slice(n * half, (n + 1) * half)
        a, b = parts[n::2]
        out[here] = own[here].astype(jnp.float32) + a[...].astype(jnp.float32) + b[...].astype(jnp.float32)


def gather_base(own, parts):
    return pl.pallas_call(
        gather_kernel,
        out_shape=jax.ShapeDtypeStruct(own.shape, jnp.float32),
        compiler_params=pltpu.CompilerParams(vmem_limit_bytes=VMEM // 4),
        cost_estimate=pl.CostEstimate(flops=0, bytes_accessed=10 * own.size, transcendentals=0),
        name="gather_base",
    )(own, *parts)


def finish_kernel(slots, base, terms, dest, out):
    drafts, rows, width = out.shape
    places = terms.shape[0]
    lane = lax.broadcasted_iota(jnp.int32, (rows, places), 1)
    where_to = dest[:, :1]
    for s in range(drafts):
        pick = jnp.where(lane == where_to + s * slots, 1.0, 0.0).astype(jnp.bfloat16)
        term = jnp.dot(pick, terms[...], preferred_element_type=jnp.float32)
        out[s] = (base[s * rows:(s + 1) * rows] + term).astype(jnp.bfloat16)


def finish(base, terms, dest, drafts, slots):
    rows = dest.shape[0]
    width = terms.shape[1]
    return pl.pallas_call(
        functools.partial(finish_kernel, slots),
        out_shape=jax.ShapeDtypeStruct((drafts, rows, width), jnp.bfloat16),
        compiler_params=pltpu.CompilerParams(vmem_limit_bytes=VMEM // 4),
        cost_estimate=pl.CostEstimate(
            flops=2 * terms.size * rows * drafts, bytes_accessed=2 * terms.size, transcendentals=0
        ),
        name="finish",
    )(base, terms, dest)


def body(
    queries,
    draft_keys,
    draft_values,
    key_cache,
    value_cache,
    lengths,
    request_adapter,
    adapter_page_table,
    output_weight,
    adapter_down,
    adapter_up,
):
    drafts, rows, width = queries.shape
    owners = lax.axis_size("dp")
    parts = lax.axis_size("tensor")
    span, rank, _ = adapter_down.shape
    slots = rows // 8
    owner_rows = -(-drafts * slots // 8) * 8
    chips = parts // 2
    swap = [(i, i ^ 1) for i in range(parts)]
    shift = lambda k: [
        (2 * x + c, 2 * ((x + k) % chips) + c) for x in range(chips) for c in range(2)
    ]
    weight_other = lax.ppermute(output_weight, "tensor", swap)
    attn, payload, dest = attend(
        queries, draft_keys, draft_values, key_cache, value_cache, lengths, request_adapter,
        adapter_page_table, slots, owner_rows, owners, span,
    )
    arrived = lax.all_to_all(
        payload.reshape(owners, owner_rows, -1), "dp", 0, 0, tiled=True
    ).reshape(owners * owner_rows, -1)
    attn = attn.reshape(drafts * rows, width)
    attn_other = lax.ppermute(attn, "tensor", swap)
    weights = (output_weight, weight_other, parts)
    far_up, far_down = project(attn, attn_other, *weights, 0, 1)
    far_up = lax.ppermute(far_up, "tensor", shift(1))
    far_down = lax.ppermute(far_down, "tensor", shift(-1))
    up, near_up, near_down, down = project(attn, attn_other, *weights, 1, 2)
    arrived, up = lax.optimization_barrier((arrived, up))
    mine = down_mix(arrived, adapter_down)
    mine, far_up, far_down = lax.optimization_barrier((mine, far_up, far_down))
    pair = (mine + lax.ppermute(mine, "tensor", swap)).astype(jnp.bfloat16)
    mixes = [pair] + [lax.ppermute(pair, "tensor", shift(k)) for k in range(1, chips)]
    terms = up_terms(mixes, arrived, adapter_up)
    terms, up, down, near_up, near_down, attn = lax.optimization_barrier(
        (terms, up, down, near_up, near_down, attn)
    )
    from_below = lax.ppermute(near_up, "tensor", shift(1))
    from_above = lax.ppermute(near_down, "tensor", shift(-1))
    up, down = merge(up, down, far_up, far_down)
    up = lax.ppermute(up, "tensor", shift(1))
    down = lax.ppermute(down, "tensor", shift(-1))
    (own,) = project(attn, attn_other, *weights, 3, 1, cuts=1)
    terms = lax.all_to_all(
        terms.reshape(owners, owner_rows, -1), "dp", 0, 0, tiled=True
    ).reshape(owners * owner_rows, -1)
    base = gather_base(own, (up, from_below, from_above, down))
    return finish(base, terms, dest, drafts, slots)


def solution(mesh):
    placed = (
        P(None, "dp", "tensor"),
        P(None, "dp", "tensor"),
        P(None, "dp", "tensor"),
        P("dp", None, "tensor"),
        P("dp", None, "tensor"),
        P("dp"),
        P("dp"),
        P(),
        P("tensor", None),
        P("dp", None, "tensor"),
        P("dp", None, "tensor"),
    )
    return jax.shard_map(
        body, mesh=mesh, in_specs=placed, out_specs=P(None, "dp", "tensor"), check_vma=False
    )
```

```python
import functools, math
import jax, jax.numpy as jnp
from jax import lax
from jax.experimental import pallas as pl
from jax.experimental.pallas import tpu as pltpu
from jax.sharding import PartitionSpec as P

LANES = 128
STEP = 16
HALF = 8
AHEAD_COPIES = 3
PIECES = 8
IN_FLIGHT = 4
AHEAD = (2, 1, 3, 0)
VMEM = 63 * 1024 * 1024

def attend_kernel(
    slots, owner_rows, span, lengths, adapters_hbm, table_hbm, q_hbm, dk_hbm, dv_hbm, k_hbm, v_hbm,
    attn, payload, dest_out, adapters, table, q, dk, dv, k, v, scores, weights, small_sems, sems,
):
    drafts, count, width = q.shape
    cache = k.shape[1]
    heads = width // LANES
    rows = drafts * heads * HALF
    scale = math.log2(math.e) / math.sqrt(LANES)
    small = [
        pltpu.make_async_copy(a, b, small_sems.at[n])
        for n, (a, b) in enumerate(
            ((q_hbm, q), (dk_hbm, dk), (dv_hbm, dv), (adapters_hbm, adapters), (table_hbm, table))
        )
    ]

    steps = count // STEP
    flow = [(0, 0), (0, 1), (0, 2)] + [p for j in range(steps - 3) for p in ((1, j), (0, j + 3))] + [(1, j) for j in range(steps - 3, steps)]

    def fetch(at):
        n, j = flow[at]
        here = pl.ds(j * STEP, STEP)
        return pltpu.make_async_copy((k_hbm, v_hbm)[n].at[here], (k, v)[n].at[here], sems.at[n, j])

    def arrive(at):
        fetch(at).wait()
        if at + AHEAD_COPIES < len(flow):
            fetch(at + AHEAD_COPIES).start()

    for copy in small:
        copy.start()
    for at in range(AHEAD_COPIES):
        fetch(at).start()

    sub = lax.broadcasted_iota(jnp.int32, (rows, cache), 0) % HALF
    lane8 = lax.broadcasted_iota(jnp.int32, (HALF, cache), 1)
    sub8 = lax.broadcasted_iota(jnp.int32, (HALF, cache), 0)
    drow = lax.broadcasted_iota(jnp.int32, (rows, drafts * HALF), 0)
    dlane = lax.broadcasted_iota(jnp.int32, (rows, drafts * HALF), 1)
    fresh_ok = (drow % HALF == dlane % HALF) & (dlane // HALF <= drow // (heads * HALF))
    for copy in small[:3]:
        copy.wait()

    def places():
        for copy in small[3:]:
            copy.wait()
        pages = table.shape[1]
        a = lax.broadcasted_iota(jnp.int32, (count, count), 0)
        b = lax.broadcasted_iota(jnp.int32, (count, count), 1)
        eye = a == b
        to_col = lambda row: jnp.sum(jnp.where(eye, jnp.broadcast_to(row, (count, count)), 0.0), axis=1, keepdims=True)
        to_row = lambda col: jnp.sum(jnp.where(eye, jnp.broadcast_to(col, (count, count)), 0.0), axis=0, keepdims=True)
        acol = to_col(adapters[...].astype(jnp.float32)).astype(jnp.int32)
        hit = acol == lax.broadcasted_iota(jnp.int32, (count, pages), 1)
        page = jnp.sum(jnp.where(hit, jnp.broadcast_to(table[...].astype(jnp.float32), (count, pages)), 0.0), axis=1, keepdims=True)
        prow = to_row(page).astype(jnp.int32)
        pcol = page.astype(jnp.int32)
        orow, ocol = prow // span, pcol // span
        rank = jnp.sum(jnp.where((ocol == orow) & (a < b), 1.0, 0.0), axis=0, keepdims=True).astype(jnp.int32)
        rank_col = jnp.sum(jnp.where((ocol == orow) & (b < a), 1.0, 0.0), axis=1, keepdims=True).astype(jnp.int32)
        last = payload.shape[0] // owner_rows - 1
        dest_out[...] = jnp.broadcast_to((last - ocol) * owner_rows + rank_col, dest_out.shape)
        dest = orow * owner_rows + rank
        local = jnp.broadcast_to((pcol - ocol * span).astype(jnp.float32), (count, LANES)).astype(jnp.bfloat16)
        return dest, local

    def score(j, carry):
        base = j * STEP
        here = pl.ds(base, STEP)
        qf = q[:, here].astype(jnp.float32)
        dkf = dk[:, here].astype(jnp.float32)
        arrive(flow.index((0, j)))
        for h in range(STEP // HALF):
            at = slice(h * HALF, (h + 1) * HALF)
            qb = jnp.concatenate([qf[s, at, g * LANES:(g + 1) * LANES] for s in range(drafts) for g in range(heads)], axis=0).astype(jnp.bfloat16)
            kb = jnp.concatenate([dkf[t, at] for t in range(drafts)], axis=0).astype(jnp.bfloat16)
            part = None
            limit = jnp.zeros((HALF, cache), jnp.int32)
            for r in range(HALF):
                one = lax.dot_general(qb, k[base + h * HALF + r], (((1,), (1,)), ((), ())), preferred_element_type=jnp.float32)
                part = one if r == 0 else jnp.where(sub == r, one, part)
                limit = jnp.where(sub8 == r, lengths[base + h * HALF + r], limit)
            seen = jnp.concatenate([(lane8 < limit).astype(jnp.int32)] * (drafts * heads), axis=0) > 0
            fresh = lax.dot_general(qb, kb, (((1,), (1,)), ((), ())), preferred_element_type=jnp.float32)
            scores[j, h, :, :cache] = jnp.where(seen, part, -1e30)
            scores[j, h, :, cache:cache + drafts * HALF] = jnp.where(fresh_ok, fresh, -1e30)
        return carry

    def soften(j, carry):
        for h in range(STEP // HALF):
            part = scores[j, h, :, :cache]
            fresh = scores[j, h, :, cache:cache + drafts * HALF]
            top = jnp.maximum(jnp.max(part, axis=1, keepdims=True), jnp.max(fresh, axis=1, keepdims=True))
            e = jnp.exp2((part - top) * scale)
            ef = jnp.exp2((fresh - top) * scale)
            inv = 1.0 / (jnp.sum(e, axis=1, keepdims=True) + jnp.sum(ef, axis=1, keepdims=True))
            weights[j, h, :, :cache] = (e * inv).astype(jnp.bfloat16)
            weights[j, h, :, cache:cache + drafts * HALF] = (ef * inv).astype(jnp.bfloat16)
        return carry

    keep = [jnp.where(sub == r, 1.0, 0.0).astype(jnp.bfloat16) for r in range(HALF)]

    def mix(j, carry):
        base = j * STEP
        here = pl.ds(base, STEP)
        dvf = dv[:, here].astype(jnp.float32)
        arrive(flow.index((1, j)))
        outs = []
        for h in range(STEP // HALF):
            at = slice(h * HALF, (h + 1) * HALF)
            vb = jnp.concatenate([dvf[t, at] for t in range(drafts)], axis=0).astype(jnp.bfloat16)
            w = weights[j, h, :, :cache]
            wf = weights[j, h, :, cache:cache + drafts * HALF]
            wide = jnp.concatenate([w * keep[r] for r in range(HALF)], axis=1)
            vals = v[pl.ds(base + h * HALF, HALF)].reshape(HALF * cache, LANES)
            mixed = jnp.dot(wide, vals, preferred_element_type=jnp.float32)
            mixed = mixed + jnp.dot(wf, vb, preferred_element_type=jnp.float32)
            outs.append(mixed)
        for s in range(drafts):
            for g in range(heads):
                at = (s * heads + g) * HALF
                piece = jnp.concatenate([o[at:at + HALF] for o in outs], axis=0).astype(jnp.bfloat16)
                attn[s, here, g * LANES:(g + 1) * LANES] = piece
        return carry

    for j in range(steps + 2):
        if j < steps:
            score(j, 0)
        if j == 1:
            dest, local = places()
        if 1 <= j <= steps:
            soften(j - 1, 0)
        if j >= 2:
            mix(j - 2, 0)

    place = lax.broadcasted_iota(jnp.int32, (payload.shape[0], count), 0)
    acc = None
    for s in range(drafts):
        pick = jnp.where(place == dest + s * slots, 1.0, 0.0).astype(jnp.bfloat16)
        part = jnp.dot(pick, jnp.concatenate([attn[s], local], axis=1), preferred_element_type=jnp.float32)
        acc = part if acc is None else acc + part
    payload[...] = acc.astype(jnp.bfloat16)


def attend(queries, draft_keys, draft_values, key_cache, value_cache, lengths, request_adapter, table, slots, owner_rows, owners, span):
    drafts, rows, width = queries.shape
    cache = key_cache.shape[1]
    vmem = pl.BlockSpec(memory_space=pltpu.VMEM)
    hbm = pl.BlockSpec(memory_space=pltpu.HBM)
    return pl.pallas_call(
        functools.partial(attend_kernel, slots, owner_rows, span),
        in_specs=[pl.BlockSpec(memory_space=pltpu.SMEM)] + [hbm] * 7,
        out_specs=[vmem] * 3,
        out_shape=[
            jax.ShapeDtypeStruct((drafts, rows, width), jnp.bfloat16),
            jax.ShapeDtypeStruct((owners * owner_rows, width + LANES), jnp.bfloat16),
            jax.ShapeDtypeStruct((rows, LANES), jnp.int32),
        ],
        scratch_shapes=[
            pltpu.VMEM((1, rows), jnp.int32),
            pltpu.VMEM((1, table.shape[0]), jnp.int32),
            pltpu.VMEM(queries.shape, jnp.bfloat16),
            pltpu.VMEM(draft_keys.shape, jnp.bfloat16),
            pltpu.VMEM(draft_values.shape, jnp.bfloat16),
            pltpu.VMEM(key_cache.shape, jnp.bfloat16),
            pltpu.VMEM(value_cache.shape, jnp.bfloat16),
            pltpu.VMEM((rows // STEP, STEP // HALF, drafts * width // LANES * HALF, cache + LANES), jnp.float32),
            pltpu.VMEM((rows // STEP, STEP // HALF, drafts * width // LANES * HALF, cache + LANES), jnp.bfloat16),
            pltpu.SemaphoreType.DMA((5,)),
            pltpu.SemaphoreType.DMA((2, rows // STEP)),
        ],
        compiler_params=pltpu.CompilerParams(vmem_limit_bytes=VMEM),
        cost_estimate=pl.CostEstimate(
            flops=8 * queries.size * cache, bytes_accessed=4 * key_cache.size, transcendentals=0
        ),
        name="attend",
    )(lengths, request_adapter.reshape(1, rows), table.reshape(1, -1), queries, draft_keys, draft_values, key_cache, value_cache)


def project_kernel(first, cuts, attn, attn_other, weight, weight_other, *refs):
    outs, (flat, held, done, sems, in_sems, out_sems) = refs[:-6], refs[-6:]
    _, rows, width = flat.shape
    place = lax.axis_index("tensor")
    chips = lax.axis_size("tensor") // 2
    blocks, sources, _, part = held.shape
    flow = [(j, n) for j in range(blocks) for n in range(sources)]
    piece = width // PIECES

    def fetch(at, s=None):
        j, n = flow[at]
        block = (place // 2 + AHEAD[first + j]) % chips * 2 + place % 2
        here = pl.ds(pl.multiple_of(block * part, part), part)
        w, to = (weight, weight_other)[n], held.at[j, n]
        if s is None:
            return pltpu.make_async_copy(w.at[:, here], to, sems.at[j, n])
        down = pl.ds(s * piece, piece)
        return pltpu.make_async_copy(w.at[down, here], to.at[down], sems.at[j, n])

    def begin(at):
        for s in range(PIECES):
            fetch(at, s).start()

    ins = [pltpu.make_async_copy(a, flat.at[n], in_sems.at[n]) for n, a in enumerate((attn, attn_other))]
    for copy in ins:
        copy.start()
    for at in range(min(IN_FLIGHT, len(flow))):
        begin(at)
    for copy in ins:
        copy.wait()
    stores = []
    for j in range(blocks):
        total = None
        for n in range(sources):
            at = j * sources + n
            fetch(at).wait()
            if at + IN_FLIGHT < len(flow):
                begin(at + IN_FLIGHT)
            part_sum = jnp.dot(flat[n], held[j, n], preferred_element_type=jnp.float32)
            total = part_sum if total is None else total + part_sum
        done[j] = total.astype(jnp.bfloat16)
        for n in range(cuts):
            at = cuts * j + n
            here = pl.ds(n * (rows // cuts), rows // cuts)
            stores.append(pltpu.make_async_copy(done.at[j, here], outs[at], out_sems.at[at]))
            stores[-1].start()
    for store in stores:
        store.wait()


def project(attn, attn_other, weight, weight_other, parts, first, blocks, cuts=2):
    rows, width = attn.shape
    part = weight.shape[1] // parts
    hbm = pl.BlockSpec(memory_space=pltpu.HBM)
    piece = jax.ShapeDtypeStruct((rows // cuts, part), jnp.bfloat16)
    return pl.pallas_call(
        functools.partial(project_kernel, first, cuts),
        in_specs=[hbm] * 4,
        out_specs=[hbm] * (cuts * blocks),
        out_shape=[piece] * (cuts * blocks),
        scratch_shapes=[
            pltpu.VMEM((2, rows, width), jnp.bfloat16),
            pltpu.VMEM((blocks, 2, width, part), jnp.bfloat16),
            pltpu.VMEM((blocks, rows, part), jnp.bfloat16),
            pltpu.SemaphoreType.DMA((blocks, 2)),
            pltpu.SemaphoreType.DMA((2,)),
            pltpu.SemaphoreType.DMA((cuts * blocks,)),
        ],
        compiler_params=pltpu.CompilerParams(vmem_limit_bytes=VMEM * 8 // 9),
        cost_estimate=pl.CostEstimate(
            flops=16 * rows * width * part * blocks,
            bytes_accessed=16 * width * part * blocks,
            transcendentals=0,
        ),
        name="project",
    )(attn, attn_other, weight, weight_other)


def merge_kernel(up, down, far_up, far_down, up_out, down_out):
    for a, b, out in ((up, far_up, up_out), (down, far_down, down_out)):
        out[...] = (a[...].astype(jnp.float32) + b[...].astype(jnp.float32)).astype(jnp.bfloat16)


def merge(up, down, far_up, far_down):
    shape = jax.ShapeDtypeStruct(up.shape, up.dtype)
    return pl.pallas_call(
        merge_kernel,
        out_shape=[shape, shape],
        compiler_params=pltpu.CompilerParams(vmem_limit_bytes=VMEM // 4),
        cost_estimate=pl.CostEstimate(flops=0, bytes_accessed=12 * up.size, transcendentals=0),
        name="merge",
    )(up, down, far_up, far_down)


def down_kernel(arrived, down, mix):
    width = down.shape[1]
    span = down.shape[0] // mix.shape[0]
    product = lax.dot_general(
        down[...], arrived[:, :width], (((1,), (1,)), ((), ())), preferred_element_type=jnp.float32
    )
    ones = jnp.ones((8, LANES), jnp.bfloat16)
    page = lax.dot_general(
        ones, arrived[:, width:], (((1,), (1,)), ((), ())), preferred_element_type=jnp.float32
    )[:1] * (1.0 / LANES)
    rank = mix.shape[0]
    total = jnp.zeros(mix.shape, jnp.float32)
    for p in range(span):
        total = total + jnp.where(page == float(p), product[p * rank:(p + 1) * rank], 0.0)
    mix[...] = total


def down_mix(arrived, down):
    rows = arrived.shape[0]
    span, rank, width = down.shape
    return pl.pallas_call(
        down_kernel,
        out_shape=jax.ShapeDtypeStruct((rank, rows), jnp.float32),
        compiler_params=pltpu.CompilerParams(vmem_limit_bytes=VMEM // 4),
        cost_estimate=pl.CostEstimate(flops=2 * rows * down.size, bytes_accessed=2 * (arrived.size + down.size), transcendentals=0),
        name="down_mix",
    )(arrived, down.reshape(span * rank, width))


def up_kernel(owner_rows, mine, one, two, three, arrived, up, out):
    rank = mine.shape[0]
    spread_width = up.shape[0]
    mix = (
        mine[...].astype(jnp.float32)
        + one[...].astype(jnp.float32)
        + two[...].astype(jnp.float32)
        + three[...].astype(jnp.float32)
    ).astype(jnp.bfloat16)
    a = lax.broadcasted_iota(jnp.int32, (rank, spread_width), 0)
    b = lax.broadcasted_iota(jnp.int32, (rank, spread_width), 1)
    repeat = jnp.where(b % rank == a, 1.0, 0.0).astype(jnp.bfloat16)
    spread = lax.dot_general(
        mix, repeat, (((0,), (0,)), ((), ())), preferred_element_type=jnp.float32
    )
    meta = arrived[...].astype(jnp.float32)
    pieces = []
    for j in range(spread_width // LANES):
        lane = lax.broadcasted_iota(jnp.int32, meta.shape, 1) + j * LANES
        same = meta == (lane // rank).astype(jnp.float32)
        pieces.append(jnp.where(same, spread[:, j * LANES:(j + 1) * LANES], 0.0).astype(jnp.bfloat16))
    terms = jnp.dot(jnp.concatenate(pieces, axis=1), up[...], preferred_element_type=jnp.float32)
    blocks = [terms[at:at + owner_rows] for at in range(0, terms.shape[0], owner_rows)]
    out[...] = jnp.concatenate(blocks[::-1], axis=0).astype(jnp.bfloat16)


def up_terms(mixes, arrived, up, owner_rows):
    rows, full = arrived.shape
    span, rank, width = up.shape
    mix_spec = pl.BlockSpec((rank, rows), lambda i: (0, 0))
    return pl.pallas_call(
        functools.partial(up_kernel, owner_rows),
        grid=(1,),
        in_specs=[mix_spec] * 4
        + [
            pl.BlockSpec((rows, LANES), lambda i: (0, full // LANES - 1)),
            pl.BlockSpec((span * rank, width), lambda i: (0, 0)),
        ],
        out_specs=pl.BlockSpec((rows, width), lambda i: (0, 0)),
        out_shape=jax.ShapeDtypeStruct((rows, width), jnp.bfloat16),
        compiler_params=pltpu.CompilerParams(vmem_limit_bytes=VMEM // 4),
        cost_estimate=pl.CostEstimate(flops=2 * rows * up.size, bytes_accessed=2 * (up.size + rows * width), transcendentals=0),
        name="up_terms",
    )(*mixes, arrived, up.reshape(span * rank, width))


def widen_kernel(own, out):
    out[...] = own[...].astype(jnp.float32)


def gather_kernel(own, *refs):
    parts, out = refs[:4], refs[4]
    half = parts[0].shape[0]
    for n in range(2):
        here = slice(n * half, (n + 1) * half)
        a, b = parts[n::2]
        out[here] = own[here] + a[...].astype(jnp.float32) + b[...].astype(jnp.float32)


def gather_base(own, parts):
    return pl.pallas_call(
        gather_kernel if parts else widen_kernel,
        out_shape=jax.ShapeDtypeStruct(own.shape, jnp.float32),
        compiler_params=pltpu.CompilerParams(vmem_limit_bytes=VMEM // 4),
        cost_estimate=pl.CostEstimate(flops=0, bytes_accessed=10 * own.size, transcendentals=0),
        name="gather_base" if parts else "widen",
    )(own, *parts)


def finish_kernel(slots, base, terms, dest, out):
    drafts, rows, width = out.shape
    places = terms.shape[0]
    lane = lax.broadcasted_iota(jnp.int32, (rows, places), 1)
    where_to = dest[:, :1]
    for s in range(drafts):
        pick = jnp.where(lane == where_to + s * slots, 1.0, 0.0).astype(jnp.bfloat16)
        term = jnp.dot(pick, terms[...], preferred_element_type=jnp.float32)
        out[s] = (base[s * rows:(s + 1) * rows] + term).astype(jnp.bfloat16)


def finish(base, terms, dest, drafts, slots):
    rows = dest.shape[0]
    width = terms.shape[1]
    return pl.pallas_call(
        functools.partial(finish_kernel, slots),
        out_shape=jax.ShapeDtypeStruct((drafts, rows, width), jnp.bfloat16),
        compiler_params=pltpu.CompilerParams(vmem_limit_bytes=VMEM // 4),
        cost_estimate=pl.CostEstimate(
            flops=2 * terms.size * rows * drafts, bytes_accessed=2 * terms.size, transcendentals=0
        ),
        name="finish",
    )(base, terms, dest)


def body(
    queries,
    draft_keys,
    draft_values,
    key_cache,
    value_cache,
    lengths,
    request_adapter,
    adapter_page_table,
    output_weight,
    adapter_down,
    adapter_up,
):
    drafts, rows, width = queries.shape
    owners = lax.axis_size("dp")
    parts = lax.axis_size("tensor")
    span, rank, _ = adapter_down.shape
    slots = rows // 8
    owner_rows = -(-drafts * slots // 8) * 8
    chips = parts // 2
    swap = [(i, i ^ 1) for i in range(parts)]
    shift = lambda k: [
        (2 * x + c, 2 * ((x + k) % chips) + c) for x in range(chips) for c in range(2)
    ]
    weight_other = lax.ppermute(output_weight, "tensor", swap)
    attn, payload, dest = attend(
        queries, draft_keys, draft_values, key_cache, value_cache, lengths, request_adapter,
        adapter_page_table, slots, owner_rows, owners, span,
    )
    arrived = lax.all_to_all(
        payload.reshape(owners, owner_rows, -1), "dp", 0, 0, tiled=True
    ).reshape(owners * owner_rows, -1)
    attn = attn.reshape(drafts * rows, width)
    attn_other = lax.ppermute(attn, "tensor", swap)
    weights = (output_weight, weight_other, parts)
    far_up, far_down = project(attn, attn_other, *weights, 0, 1)
    far_up = lax.ppermute(far_up, "tensor", shift(1))
    far_down = lax.ppermute(far_down, "tensor", shift(-1))
    up, near_up, near_down, down = project(attn, attn_other, *weights, 1, 2)
    arrived, up = lax.optimization_barrier((arrived, up))
    mine = down_mix(arrived, adapter_down)
    mine, far_up, far_down = lax.optimization_barrier((mine, far_up, far_down))
    pair = (mine + lax.ppermute(mine, "tensor", swap)).astype(jnp.bfloat16)
    mixes = [pair] + [lax.ppermute(pair, "tensor", shift(k)) for k in range(1, chips)]
    terms = up_terms(mixes, arrived, adapter_up, owner_rows)
    terms, up, down, near_up, near_down, attn = lax.optimization_barrier(
        (terms, up, down, near_up, near_down, attn)
    )
    from_below = lax.ppermute(near_up, "tensor", shift(1))
    from_above = lax.ppermute(near_down, "tensor", shift(-1))
    up, down = merge(up, down, far_up, far_down)
    up = lax.ppermute(up, "tensor", shift(1))
    down = lax.ppermute(down, "tensor", shift(-1))
    (own,) = project(attn, attn_other, *weights, 3, 1, cuts=1)
    terms = lax.all_to_all(
        terms.reshape(owners, owner_rows, -1), "dp", 0, 0, tiled=True,
        axis_index_groups=[list(range(owners))[::-1]],
    ).reshape(owners * owner_rows, -1)
    base = gather_base(gather_base(own, ()), (up, from_below, from_above, down))
    return finish(base, terms, dest, drafts, slots)


def solution(mesh):
    placed = (
        P(None, "dp", "tensor"),
        P(None, "dp", "tensor"),
        P(None, "dp", "tensor"),
        P("dp", None, "tensor"),
        P("dp", None, "tensor"),
        P("dp"),
        P("dp"),
        P(),
        P("tensor", None),
        P("dp", None, "tensor"),
        P("dp", None, "tensor"),
    )
    return jax.shard_map(
        body, mesh=mesh, in_specs=placed, out_specs=P(None, "dp", "tensor"), check_vma=False
    )
```

```python
import functools, math
import jax, jax.numpy as jnp
from jax import lax
from jax.experimental import pallas as pl
from jax.experimental.pallas import tpu as pltpu
from jax.sharding import PartitionSpec as P

LANES = 128
STEP = 16
HALF = 8
AHEAD_COPIES = 3
PIECES = 8
IN_FLIGHT = 4
AHEAD = (2, 1, 3, 0)
VMEM = 63 * 1024 * 1024

def attend_kernel(
    slots, owner_rows, span, lengths, adapters_hbm, table_hbm, q_hbm, dk_hbm, dv_hbm, k_hbm, v_hbm,
    attn, payload, dest_out, adapters, table, q, dk, dv, k, v, scores, weights, small_sems, sems,
):
    drafts, count, width = q.shape
    cache = k.shape[1]
    heads = width // LANES
    rows = drafts * heads * HALF
    scale = math.log2(math.e) / math.sqrt(LANES)
    small = [
        pltpu.make_async_copy(a, b, small_sems.at[n])
        for n, (a, b) in enumerate(
            ((q_hbm, q), (dk_hbm, dk), (dv_hbm, dv), (adapters_hbm, adapters), (table_hbm, table))
        )
    ]

    steps = count // STEP
    flow = [(0, 0), (0, 1), (0, 2)] + [p for j in range(steps - 3) for p in ((1, j), (0, j + 3))] + [(1, j) for j in range(steps - 3, steps)]

    def fetch(at):
        n, j = flow[at]
        here = pl.ds(j * STEP, STEP)
        return pltpu.make_async_copy((k_hbm, v_hbm)[n].at[here], (k, v)[n].at[here], sems.at[n, j])

    def arrive(at):
        fetch(at).wait()
        if at + AHEAD_COPIES < len(flow):
            fetch(at + AHEAD_COPIES).start()

    for copy in small:
        copy.start()
    for at in range(AHEAD_COPIES):
        fetch(at).start()

    sub = lax.broadcasted_iota(jnp.int32, (rows, cache), 0) % HALF
    lane8 = lax.broadcasted_iota(jnp.int32, (HALF, cache), 1)
    sub8 = lax.broadcasted_iota(jnp.int32, (HALF, cache), 0)
    drow = lax.broadcasted_iota(jnp.int32, (rows, drafts * HALF), 0)
    dlane = lax.broadcasted_iota(jnp.int32, (rows, drafts * HALF), 1)
    fresh_ok = (drow % HALF == dlane % HALF) & (dlane // HALF <= drow // (heads * HALF))
    for copy in small[:3]:
        copy.wait()

    def places():
        for copy in small[3:]:
            copy.wait()
        pages = table.shape[1]
        a = lax.broadcasted_iota(jnp.int32, (count, count), 0)
        b = lax.broadcasted_iota(jnp.int32, (count, count), 1)
        eye = a == b
        to_col = lambda row: jnp.sum(jnp.where(eye, jnp.broadcast_to(row, (count, count)), 0.0), axis=1, keepdims=True)
        to_row = lambda col: jnp.sum(jnp.where(eye, jnp.broadcast_to(col, (count, count)), 0.0), axis=0, keepdims=True)
        acol = to_col(adapters[...].astype(jnp.float32)).astype(jnp.int32)
        hit = acol == lax.broadcasted_iota(jnp.int32, (count, pages), 1)
        page = jnp.sum(jnp.where(hit, jnp.broadcast_to(table[...].astype(jnp.float32), (count, pages)), 0.0), axis=1, keepdims=True)
        prow = to_row(page).astype(jnp.int32)
        pcol = page.astype(jnp.int32)
        orow, ocol = prow // span, pcol // span
        rank = jnp.sum(jnp.where((ocol == orow) & (a < b), 1.0, 0.0), axis=0, keepdims=True).astype(jnp.int32)
        rank_col = jnp.sum(jnp.where((ocol == orow) & (b < a), 1.0, 0.0), axis=1, keepdims=True).astype(jnp.int32)
        last = payload.shape[0] // owner_rows - 1
        dest_out[...] = jnp.broadcast_to((last - ocol) * owner_rows + rank_col, dest_out.shape)
        dest = orow * owner_rows + rank
        local = jnp.broadcast_to((pcol - ocol * span).astype(jnp.float32), (count, LANES)).astype(jnp.bfloat16)
        return dest, local

    def score(j, carry):
        base = j * STEP
        here = pl.ds(base, STEP)
        qf = q[:, here].astype(jnp.float32)
        dkf = dk[:, here].astype(jnp.float32)
        arrive(flow.index((0, j)))
        for h in range(STEP // HALF):
            at = slice(h * HALF, (h + 1) * HALF)
            qb = jnp.concatenate([qf[s, at, g * LANES:(g + 1) * LANES] for s in range(drafts) for g in range(heads)], axis=0).astype(jnp.bfloat16)
            kb = jnp.concatenate([dkf[t, at] for t in range(drafts)], axis=0).astype(jnp.bfloat16)
            part = None
            limit = jnp.zeros((HALF, cache), jnp.int32)
            for r in range(HALF):
                one = lax.dot_general(qb, k[base + h * HALF + r], (((1,), (1,)), ((), ())), preferred_element_type=jnp.float32)
                part = one if r == 0 else jnp.where(sub == r, one, part)
                limit = jnp.where(sub8 == r, lengths[base + h * HALF + r], limit)
            seen = jnp.concatenate([(lane8 < limit).astype(jnp.int32)] * (drafts * heads), axis=0) > 0
            fresh = lax.dot_general(qb, kb, (((1,), (1,)), ((), ())), preferred_element_type=jnp.float32)
            scores[j, h, :, :cache] = jnp.where(seen, part, -1e30)
            scores[j, h, :, cache:cache + drafts * HALF] = jnp.where(fresh_ok, fresh, -1e30)
        return carry

    def soften(j, carry):
        for h in range(STEP // HALF):
            part = scores[j, h, :, :cache]
            fresh = scores[j, h, :, cache:cache + drafts * HALF]
            top = jnp.maximum(jnp.max(part, axis=1, keepdims=True), jnp.max(fresh, axis=1, keepdims=True))
            e = jnp.exp2((part - top) * scale)
            ef = jnp.exp2((fresh - top) * scale)
            inv = 1.0 / (jnp.sum(e, axis=1, keepdims=True) + jnp.sum(ef, axis=1, keepdims=True))
            weights[j, h, :, :cache] = (e * inv).astype(jnp.bfloat16)
            weights[j, h, :, cache:cache + drafts * HALF] = (ef * inv).astype(jnp.bfloat16)
        return carry

    keep = [jnp.where(sub == r, 1.0, 0.0).astype(jnp.bfloat16) for r in range(HALF)]

    def mix(j, carry):
        base = j * STEP
        here = pl.ds(base, STEP)
        dvf = dv[:, here].astype(jnp.float32)
        arrive(flow.index((1, j)))
        outs = []
        for h in range(STEP // HALF):
            at = slice(h * HALF, (h + 1) * HALF)
            vb = jnp.concatenate([dvf[t, at] for t in range(drafts)], axis=0).astype(jnp.bfloat16)
            w = weights[j, h, :, :cache]
            wf = weights[j, h, :, cache:cache + drafts * HALF]
            wide = jnp.concatenate([w * keep[r] for r in range(HALF)], axis=1)
            vals = v[pl.ds(base + h * HALF, HALF)].reshape(HALF * cache, LANES)
            mixed = jnp.dot(wide, vals, preferred_element_type=jnp.float32)
            mixed = mixed + jnp.dot(wf, vb, preferred_element_type=jnp.float32)
            outs.append(mixed)
        for s in range(drafts):
            for g in range(heads):
                at = (s * heads + g) * HALF
                piece = jnp.concatenate([o[at:at + HALF] for o in outs], axis=0).astype(jnp.bfloat16)
                attn[s, here, g * LANES:(g + 1) * LANES] = piece
        return carry

    for j in range(steps + 2):
        if j < steps:
            score(j, 0)
        if j == 1:
            dest, local = places()
        if 1 <= j <= steps:
            soften(j - 1, 0)
        if j >= 2:
            mix(j - 2, 0)

    place = lax.broadcasted_iota(jnp.int32, (payload.shape[0], count), 0)
    acc = None
    for s in range(drafts):
        pick = jnp.where(place == dest + s * slots, 1.0, 0.0).astype(jnp.bfloat16)
        part = jnp.dot(pick, jnp.concatenate([attn[s], local], axis=1), preferred_element_type=jnp.float32)
        acc = part if acc is None else acc + part
    payload[...] = acc.astype(jnp.bfloat16)


def attend(queries, draft_keys, draft_values, key_cache, value_cache, lengths, request_adapter, table, slots, owner_rows, owners, span):
    drafts, rows, width = queries.shape
    cache = key_cache.shape[1]
    vmem = pl.BlockSpec(memory_space=pltpu.VMEM)
    hbm = pl.BlockSpec(memory_space=pltpu.HBM)
    return pl.pallas_call(
        functools.partial(attend_kernel, slots, owner_rows, span),
        in_specs=[pl.BlockSpec(memory_space=pltpu.SMEM)] + [hbm] * 7,
        out_specs=[vmem] * 3,
        out_shape=[
            jax.ShapeDtypeStruct((drafts, rows, width), jnp.bfloat16),
            jax.ShapeDtypeStruct((owners * owner_rows, width + LANES), jnp.bfloat16),
            jax.ShapeDtypeStruct((rows, LANES), jnp.int32),
        ],
        scratch_shapes=[
            pltpu.VMEM((1, rows), jnp.int32),
            pltpu.VMEM((1, table.shape[0]), jnp.int32),
            pltpu.VMEM(queries.shape, jnp.bfloat16),
            pltpu.VMEM(draft_keys.shape, jnp.bfloat16),
            pltpu.VMEM(draft_values.shape, jnp.bfloat16),
            pltpu.VMEM(key_cache.shape, jnp.bfloat16),
            pltpu.VMEM(value_cache.shape, jnp.bfloat16),
            pltpu.VMEM((rows // STEP, STEP // HALF, drafts * width // LANES * HALF, cache + LANES), jnp.float32),
            pltpu.VMEM((rows // STEP, STEP // HALF, drafts * width // LANES * HALF, cache + LANES), jnp.bfloat16),
            pltpu.SemaphoreType.DMA((5,)),
            pltpu.SemaphoreType.DMA((2, rows // STEP)),
        ],
        compiler_params=pltpu.CompilerParams(vmem_limit_bytes=VMEM),
        cost_estimate=pl.CostEstimate(
            flops=8 * queries.size * cache, bytes_accessed=4 * key_cache.size, transcendentals=0
        ),
        name="attend",
    )(lengths, request_adapter.reshape(1, rows), table.reshape(1, -1), queries, draft_keys, draft_values, key_cache, value_cache)


def project_kernel(first, cuts, attn, attn_other, weight, weight_other, *refs):
    outs, (flat, held, done, sems, in_sems, out_sems) = refs[:-6], refs[-6:]
    _, rows, width = flat.shape
    place = lax.axis_index("tensor")
    chips = lax.axis_size("tensor") // 2
    blocks, sources, _, part = held.shape
    flow = [(j, n) for j in range(blocks) for n in range(sources)]
    piece = width // PIECES

    def fetch(at, s=None):
        j, n = flow[at]
        block = (place // 2 + AHEAD[first + j]) % chips * 2 + place % 2
        here = pl.ds(pl.multiple_of(block * part, part), part)
        w, to = (weight, weight_other)[n], held.at[j, n]
        if s is None:
            return pltpu.make_async_copy(w.at[:, here], to, sems.at[j, n])
        down = pl.ds(s * piece, piece)
        return pltpu.make_async_copy(w.at[down, here], to.at[down], sems.at[j, n])

    def begin(at):
        for s in range(PIECES):
            fetch(at, s).start()

    ins = [pltpu.make_async_copy(a, flat.at[n], in_sems.at[n]) for n, a in enumerate((attn, attn_other))]
    for copy in ins:
        copy.start()
    for at in range(min(IN_FLIGHT, len(flow))):
        begin(at)
    for copy in ins:
        copy.wait()
    stores = []
    for j in range(blocks):
        total = None
        for n in range(sources):
            at = j * sources + n
            fetch(at).wait()
            if at + IN_FLIGHT < len(flow):
                begin(at + IN_FLIGHT)
            part_sum = jnp.dot(flat[n], held[j, n], preferred_element_type=jnp.float32)
            total = part_sum if total is None else total + part_sum
        done[j] = total.astype(jnp.bfloat16)
        for n in range(cuts):
            at = cuts * j + n
            here = pl.ds(n * (rows // cuts), rows // cuts)
            stores.append(pltpu.make_async_copy(done.at[j, here], outs[at], out_sems.at[at]))
            stores[-1].start()
    for store in stores:
        store.wait()


def project(attn, attn_other, weight, weight_other, parts, first, blocks, cuts=2):
    rows, width = attn.shape
    part = weight.shape[1] // parts
    hbm = pl.BlockSpec(memory_space=pltpu.HBM)
    piece = jax.ShapeDtypeStruct((rows // cuts, part), jnp.bfloat16)
    return pl.pallas_call(
        functools.partial(project_kernel, first, cuts),
        in_specs=[hbm] * 4,
        out_specs=[hbm] * (cuts * blocks),
        out_shape=[piece] * (cuts * blocks),
        scratch_shapes=[
            pltpu.VMEM((2, rows, width), jnp.bfloat16),
            pltpu.VMEM((blocks, 2, width, part), jnp.bfloat16),
            pltpu.VMEM((blocks, rows, part), jnp.bfloat16),
            pltpu.SemaphoreType.DMA((blocks, 2)),
            pltpu.SemaphoreType.DMA((2,)),
            pltpu.SemaphoreType.DMA((cuts * blocks,)),
        ],
        compiler_params=pltpu.CompilerParams(vmem_limit_bytes=VMEM * 8 // 9),
        cost_estimate=pl.CostEstimate(
            flops=16 * rows * width * part * blocks,
            bytes_accessed=16 * width * part * blocks,
            transcendentals=0,
        ),
        name="project",
    )(attn, attn_other, weight, weight_other)


def merge_kernel(up, down, far_up, far_down, up_out, down_out):
    for a, b, out in ((up, far_up, up_out), (down, far_down, down_out)):
        out[...] = (a[...].astype(jnp.float32) + b[...].astype(jnp.float32)).astype(jnp.bfloat16)


def merge(up, down, far_up, far_down):
    shape = jax.ShapeDtypeStruct(up.shape, up.dtype)
    return pl.pallas_call(
        merge_kernel,
        out_shape=[shape, shape],
        compiler_params=pltpu.CompilerParams(vmem_limit_bytes=VMEM // 4),
        cost_estimate=pl.CostEstimate(flops=0, bytes_accessed=12 * up.size, transcendentals=0),
        name="merge",
    )(up, down, far_up, far_down)


def down_kernel(arrived, down, mix):
    width = down.shape[1]
    span = down.shape[0] // mix.shape[0]
    product = lax.dot_general(
        down[...], arrived[:, :width], (((1,), (1,)), ((), ())), preferred_element_type=jnp.float32
    )
    ones = jnp.ones((8, LANES), jnp.bfloat16)
    page = lax.dot_general(
        ones, arrived[:, width:], (((1,), (1,)), ((), ())), preferred_element_type=jnp.float32
    )[:1] * (1.0 / LANES)
    rank = mix.shape[0]
    total = jnp.zeros(mix.shape, jnp.float32)
    for p in range(span):
        total = total + jnp.where(page == float(p), product[p * rank:(p + 1) * rank], 0.0)
    mix[...] = total


def down_mix(arrived, down):
    rows = arrived.shape[0]
    span, rank, width = down.shape
    return pl.pallas_call(
        down_kernel,
        out_shape=jax.ShapeDtypeStruct((rank, rows), jnp.float32),
        compiler_params=pltpu.CompilerParams(vmem_limit_bytes=VMEM // 4),
        cost_estimate=pl.CostEstimate(flops=2 * rows * down.size, bytes_accessed=2 * (arrived.size + down.size), transcendentals=0),
        name="down_mix",
    )(arrived, down.reshape(span * rank, width))


def up_kernel(owner_rows, mine, one, two, three, arrived, up, out):
    rank = mine.shape[0]
    spread_width = up.shape[0]
    mix = (
        mine[...].astype(jnp.float32)
        + one[...].astype(jnp.float32)
        + two[...].astype(jnp.float32)
        + three[...].astype(jnp.float32)
    ).astype(jnp.bfloat16)
    a = lax.broadcasted_iota(jnp.int32, (rank, spread_width), 0)
    b = lax.broadcasted_iota(jnp.int32, (rank, spread_width), 1)
    repeat = jnp.where(b % rank == a, 1.0, 0.0).astype(jnp.bfloat16)
    spread = lax.dot_general(
        mix, repeat, (((0,), (0,)), ((), ())), preferred_element_type=jnp.float32
    )
    meta = arrived[...].astype(jnp.float32)
    pieces = []
    for j in range(spread_width // LANES):
        lane = lax.broadcasted_iota(jnp.int32, meta.shape, 1) + j * LANES
        same = meta == (lane // rank).astype(jnp.float32)
        pieces.append(jnp.where(same, spread[:, j * LANES:(j + 1) * LANES], 0.0).astype(jnp.bfloat16))
    terms = jnp.dot(jnp.concatenate(pieces, axis=1), up[...], preferred_element_type=jnp.float32)
    blocks = [terms[at:at + owner_rows] for at in range(0, terms.shape[0], owner_rows)]
    out[...] = jnp.concatenate(blocks[::-1], axis=0).astype(jnp.bfloat16)


def up_terms(mixes, arrived, up, owner_rows):
    rows, full = arrived.shape
    span, rank, width = up.shape
    mix_spec = pl.BlockSpec((rank, rows), lambda i: (0, 0))
    return pl.pallas_call(
        functools.partial(up_kernel, owner_rows),
        grid=(1,),
        in_specs=[mix_spec] * 4
        + [
            pl.BlockSpec((rows, LANES), lambda i: (0, full // LANES - 1)),
            pl.BlockSpec((span * rank, width), lambda i: (0, 0)),
        ],
        out_specs=pl.BlockSpec((rows, width), lambda i: (0, 0)),
        out_shape=jax.ShapeDtypeStruct((rows, width), jnp.bfloat16),
        compiler_params=pltpu.CompilerParams(vmem_limit_bytes=VMEM // 4),
        cost_estimate=pl.CostEstimate(flops=2 * rows * up.size, bytes_accessed=2 * (up.size + rows * width), transcendentals=0),
        name="up_terms",
    )(*mixes, arrived, up.reshape(span * rank, width))


def widen_kernel(own, out):
    out[...] = own[...].astype(jnp.float32)


def gather_kernel(own, *refs):
    parts, out = refs[:4], refs[4]
    half = parts[0].shape[0]
    for n in range(2):
        here = slice(n * half, (n + 1) * half)
        a, b = parts[n::2]
        out[here] = own[here] + a[...].astype(jnp.float32) + b[...].astype(jnp.float32)


def gather_base(own, parts):
    return pl.pallas_call(
        gather_kernel if parts else widen_kernel,
        out_shape=jax.ShapeDtypeStruct(own.shape, jnp.float32),
        compiler_params=pltpu.CompilerParams(vmem_limit_bytes=VMEM // 4),
        cost_estimate=pl.CostEstimate(flops=0, bytes_accessed=10 * own.size, transcendentals=0),
        name="gather_base" if parts else "widen",
    )(own, *parts)


def finish_kernel(slots, base, terms, dest, out):
    drafts, rows, width = out.shape
    places = terms.shape[0]
    lane = lax.broadcasted_iota(jnp.int32, (rows, places), 1)
    where_to = dest[:, :1]
    for s in range(drafts):
        pick = jnp.where(lane == where_to + s * slots, 1.0, 0.0).astype(jnp.bfloat16)
        term = jnp.dot(pick, terms[...], preferred_element_type=jnp.float32)
        out[s] = (base[s * rows:(s + 1) * rows] + term).astype(jnp.bfloat16)


def finish(base, terms, dest, drafts, slots):
    rows = dest.shape[0]
    width = terms.shape[1]
    return pl.pallas_call(
        functools.partial(finish_kernel, slots),
        out_shape=jax.ShapeDtypeStruct((drafts, rows, width), jnp.bfloat16),
        compiler_params=pltpu.CompilerParams(vmem_limit_bytes=VMEM // 4),
        cost_estimate=pl.CostEstimate(
            flops=2 * terms.size * rows * drafts, bytes_accessed=2 * terms.size, transcendentals=0
        ),
        name="finish",
    )(base, terms, dest)


def body(
    queries,
    draft_keys,
    draft_values,
    key_cache,
    value_cache,
    lengths,
    request_adapter,
    adapter_page_table,
    output_weight,
    adapter_down,
    adapter_up,
):
    drafts, rows, width = queries.shape
    owners = lax.axis_size("dp")
    parts = lax.axis_size("tensor")
    span, rank, _ = adapter_down.shape
    slots = rows // 8
    owner_rows = -(-drafts * slots // 8) * 8
    chips = parts // 2
    swap = [(i, i ^ 1) for i in range(parts)]
    shift = lambda k: [
        (2 * x + c, 2 * ((x + k) % chips) + c) for x in range(chips) for c in range(2)
    ]
    weight_other = lax.ppermute(output_weight, "tensor", swap)
    attn, payload, dest = attend(
        queries, draft_keys, draft_values, key_cache, value_cache, lengths, request_adapter,
        adapter_page_table, slots, owner_rows, owners, span,
    )
    arrived = lax.all_to_all(
        payload.reshape(owners, owner_rows, -1), "dp", 0, 0, tiled=True
    ).reshape(owners * owner_rows, -1)
    attn = attn.reshape(drafts * rows, width)
    attn_other = lax.ppermute(attn, "tensor", swap)
    weights = (output_weight, weight_other, parts)
    far_up, far_down = project(attn, attn_other, *weights, 0, 1)
    far_up = lax.ppermute(far_up, "tensor", shift(1))
    far_down = lax.ppermute(far_down, "tensor", shift(-1))
    up, near_up, near_down, down = project(attn, attn_other, *weights, 1, 2)
    arrived, up = lax.optimization_barrier((arrived, up))
    mine = down_mix(arrived, adapter_down)
    mine, far_up, far_down = lax.optimization_barrier((mine, far_up, far_down))
    pair = (mine + lax.ppermute(mine, "tensor", swap)).astype(jnp.bfloat16)
    mixes = [pair] + [lax.ppermute(pair, "tensor", shift(k)) for k in range(chips - 1, 0, -1)]
    terms = up_terms(mixes, arrived, adapter_up, owner_rows)
    terms, up, down, near_up, near_down, attn = lax.optimization_barrier(
        (terms, up, down, near_up, near_down, attn)
    )
    from_below = lax.ppermute(near_up, "tensor", shift(1))
    from_above = lax.ppermute(near_down, "tensor", shift(-1))
    up, down = merge(up, down, far_up, far_down)
    up = lax.ppermute(up, "tensor", shift(1))
    down = lax.ppermute(down, "tensor", shift(-1))
    (own,) = project(attn, attn_other, *weights, 3, 1, cuts=1)
    terms = lax.all_to_all(
        terms.reshape(owners, owner_rows, -1), "dp", 0, 0, tiled=True,
        axis_index_groups=[list(range(owners))[::-1]],
    ).reshape(owners * owner_rows, -1)
    base = gather_base(gather_base(own, ()), (up, from_below, from_above, down))
    return finish(base, terms, dest, drafts, slots)


def solution(mesh):
    placed = (
        P(None, "dp", "tensor"),
        P(None, "dp", "tensor"),
        P(None, "dp", "tensor"),
        P("dp", None, "tensor"),
        P("dp", None, "tensor"),
        P("dp"),
        P("dp"),
        P(),
        P("tensor", None),
        P("dp", None, "tensor"),
        P("dp", None, "tensor"),
    )
    return jax.shard_map(
        body, mesh=mesh, in_specs=placed, out_specs=P(None, "dp", "tensor"), check_vma=False
    )
```
